32 devices in a mesh: feat: 4 (over y, core), dom: 8 (over z, x).
Axes of the slice: x: 2, y: 2, z: 4, core: 2. Of those that a mesh axis runs over, the one named last changes fastest.
Arguments:
- features: bfloat16 [4, 1024, 4096], P(None, 'dom', 'feat'), may hold values from -6 to 6
- w_one: bfloat16 [4096, 1024], P('feat'), may hold values from -0.09375 to 0.09375
- w_two: bfloat16 [1024, 512], replicated, may hold values from -0.25 to 0.25
- neighbor: int32 [4, 1024, 10], P('feat', 'dom'), may hold values from 0 to 191
- degree: int32 [4, 1024], P('feat', 'dom'), may hold values from 1 to 10
- send_rows: int32 [4, 64, 8], P('feat', 'dom'), may hold values from 0 to 127
- grad_out: bfloat16 [4, 1024, 512], P('feat', 'dom'), may hold values from -6 to 6
Outputs:
- out_two: bfloat16 [4, 1024, 512], P('feat', 'dom')
- grad_one: float32 [4096, 1024], P('feat')
- grad_two: float32 [1024, 512], replicated
The draws below stay inside these ranges and needn't reach their ends.
All inputs are finite; a program needn't handle non-finite values.
Results may differ from the reference program's by a relative error of at most 0.015.
Values may be sent and summed in bfloat16 or wider, within the bound.
A program may use at most 64 MiB of HBM per device.

```python
import math
import jax
import jax.numpy as jnp
from jax import lax

D = 4096
HID = 512
FANOUT = 10
NODES_DEV = 128
KMAX = 8
NODES = 4096
N_FEAT = 4
N_DOM = 8


def place_ends(drawn, own_key, smallest, top_value):
    longest = drawn.shape.index(max(drawn.shape))
    spots = []
    for shift in (0, 1):
        where = [jax.random.randint(jax.random.fold_in(own_key, axis), (), 0, length) for axis, length in enumerate(drawn.shape)]
        where[longest] = (where[longest] + shift) % drawn.shape[longest]
        spots.append(tuple(where))
    return drawn.at[spots[0]].set(smallest).at[spots[1]].set(top_value)


def steps_of(stream_key, shape, cuts, least, largest):
    loudness, own = 1.0, jax.random.fold_in(stream_key, 6)
    for axis_at, shards_of in cuts:
        steps = jnp.exp(jax.random.uniform(jax.random.fold_in(own, axis_at), (shards_of,), jnp.float32, least / len(cuts), largest / len(cuts)))
        loudness = loudness * jnp.repeat(steps, shape[axis_at] // shards_of).reshape([-1 if axis == axis_at else 1 for axis in range(len(shape))])
    return loudness


def gaussian(stream_key, dims, deviation, limit, pieces=(), kind=jnp.bfloat16):
    array = deviation * jax.random.normal(stream_key, dims, jnp.float32)
    if pieces:
        array = array * steps_of(stream_key, dims, pieces, -0.22, 0.18)
    return jnp.clip(array, -limit, limit).astype(kind)


def setup_inputs(seed: int = 0) -> dict:
    keys = jax.random.split(jax.random.key(seed), 8)
    return {
        "features": gaussian(keys[0], (N_FEAT, N_DOM * NODES_DEV, D), 1.0, 6.0, ((1, 8), (2, 4))),
        "w_one": gaussian(keys[1], (D, 2 * HID), D ** -0.5, 0.09375, ((0, 4),)),
        "w_two": gaussian(keys[2], (2 * HID, HID), HID ** -0.5, 0.25),
        "neighbor": place_ends(jax.random.randint(keys[3], (N_FEAT, N_DOM * NODES_DEV, FANOUT), 0, NODES_DEV + N_DOM * KMAX), jax.random.fold_in(keys[3], 1), 0, (NODES_DEV + N_DOM * KMAX) - 1).astype(jnp.int32),
        "degree": place_ends(jax.random.randint(keys[4], (N_FEAT, N_DOM * NODES_DEV), 1, FANOUT + 1), jax.random.fold_in(keys[4], 1), 1, FANOUT).astype(jnp.int32),
        "send_rows": place_ends(jax.random.randint(keys[5], (N_FEAT, N_DOM * N_DOM, KMAX), 0, NODES_DEV), jax.random.fold_in(keys[5], 1), 0, NODES_DEV - 1).astype(jnp.int32),
        "grad_out": gaussian(keys[6], (N_FEAT, N_DOM * NODES_DEV, HID), 1.0, 6.0, ((0, 4), (1, 8))),
    }


def mean_weights(degree):
    slots = jnp.arange(FANOUT, dtype=jnp.int32)
    used = (slots[None, None, :] < degree[:, :, None]).astype(jnp.float32)
    return used / degree[:, :, None].astype(jnp.float32)

def spread(values, neighbor, weight, sends):
    width = values.shape[-1]
    boxes = jax.vmap(lambda rows, index: rows[index])(values, sends)
    recv = jnp.swapaxes(boxes, 0, 1).reshape(N_DOM, N_DOM * KMAX, width)
    table = jnp.concatenate([values, recv], axis=1)
    gathered = jax.vmap(lambda rows, index: rows[index])(table, neighbor)
    return lax.optimization_barrier(jnp.sum(gathered.astype(jnp.float32) * weight[..., None], axis=2))

def gather_back(grads, neighbor, weight, sends):
    width = grads.shape[-1]
    terms = weight[..., None] * grads[:, :, None, :]

    def collect(index, vals):
        empty = jnp.zeros((NODES_DEV + N_DOM * KMAX, width), jnp.float32)
        return empty.at[index.reshape(-1)].add(vals.reshape(-1, width))
    table = jax.vmap(collect)(neighbor, terms)
    local = table[:, :NODES_DEV]
    slots = table[:, NODES_DEV:].astype(jnp.bfloat16).reshape(N_DOM, N_DOM, KMAX, width)
    returned = jnp.swapaxes(slots, 0, 1)

    def home(index, vals):
        empty = jnp.zeros((NODES_DEV, width), jnp.float32)
        return empty.at[index.reshape(-1)].add(vals.reshape(-1, width).astype(jnp.float32))
    return local + jax.vmap(home)(sends, returned)

def reference(features, w_one, w_two, neighbor, degree, send_rows, grad_out):

    def group(items):
        feats, nbrs, degs, sends, grads = items
        nbrs = nbrs.reshape(N_DOM, NODES_DEV, FANOUT)
        degs = degs.reshape(N_DOM, NODES_DEV)
        sends = sends.reshape(N_DOM, N_DOM, KMAX)
        weight = mean_weights(degs)
        proj = jnp.dot(feats, w_one, preferred_element_type=jnp.float32).reshape(N_DOM, NODES_DEV, 2 * HID)
        p_self = proj[..., :HID]
        p_near = proj[..., HID:].astype(jnp.bfloat16)
        pre = p_self + spread(p_near, nbrs, weight, sends)
        hidden = (pre * jax.nn.sigmoid(pre)).astype(jnp.bfloat16)
        agg = spread(hidden, nbrs, weight, sends).astype(jnp.bfloat16)
        joined = jnp.concatenate([hidden, agg], axis=-1).reshape(N_DOM * NODES_DEV, 2 * HID)
        out = jnp.dot(joined, w_two, preferred_element_type=jnp.float32).astype(jnp.bfloat16)
        two_sum = jnp.dot(joined.T, grads, preferred_element_type=jnp.float32)
        dcat = jnp.dot(grads, w_two.T, preferred_element_type=jnp.float32).reshape(N_DOM, NODES_DEV, 2 * HID)
        d_hidden = dcat[..., :HID] + gather_back(dcat[..., HID:], nbrs, weight, sends)
        sig = jax.nn.sigmoid(pre)
        d_pre = d_hidden * sig * (1.0 + pre * (1.0 - sig))
        d_near = gather_back(d_pre, nbrs, weight, sends)
        d_proj = jnp.concatenate([d_pre, d_near], axis=-1).astype(jnp.bfloat16).reshape(N_DOM * NODES_DEV, 2 * HID)
        one_sum = jnp.dot(feats.T, d_proj, preferred_element_type=jnp.float32)
        return (out, one_sum, two_sum)
    outs, one_sums, two_sums = lax.map(group, (features, neighbor, degree, send_rows, grad_out))
    scale = 1.0 / math.sqrt(NODES)
    return (outs, lax.optimization_barrier(jnp.sum(one_sums, axis=0)) * scale, lax.optimization_barrier(jnp.sum(two_sums, axis=0)) * scale)
```

```python
import functools
import math

import jax
import jax.numpy as jnp
from jax import lax
from jax.experimental import pallas as pl
from jax.experimental.pallas import tpu as pltpu
from jax.sharding import PartitionSpec as P

BF = jnp.bfloat16
F32 = jnp.float32
SLOT = 16
TILE = 256


def dot(a, b):
    return jnp.dot(a, b, preferred_element_type=F32)


def dot_nt(a, b):
    return lax.dot_general(a, b, (((1,), (1,)), ((), ())), preferred_element_type=F32)


def kernel(
    feat, nx, nz, kmax,
    feats, w_one, w_two, nbr, inv, sidx, grads,
    out, one, two,
    proj, projb, r1, q, qb, r2, cm, ct, sm, st, t1, t2, b1, b2, k0, k1, h0, h1,
    dcs, dh, pself, dnl, joined, ft, dp, g, rx, sx, rz, ts, u1, ub, u2, v, vx, vs, vz,
    ssem, rsem,
):
    ny = feat // 2
    parts = nx * nz
    n = nbr.shape[0]
    w = grads.shape[1]
    cols = w_one.shape[0]
    fan = nbr.shape[1]
    fi = lax.axis_index("feat")
    di = lax.axis_index("dom")
    y, c = fi // 2, fi % 2
    z, x = di // nx, di % nx
    mate = (y * 2 + 1 - c, di)
    count = [0]

    def send(src, dst, device):
        k = count[0]
        count[0] += 1
        copy = pltpu.make_async_remote_copy(
            src_ref=src, dst_ref=dst, send_sem=ssem.at[k], recv_sem=rsem.at[k],
            device_id=device, device_id_type=pl.DeviceIdType.MESH,
        )
        copy.start()
        copies.append(copy)
        return copy

    copies = []
    ypeers = [(lax.rem(y + o, ny) * 2 + c, di) for o in range(1, ny)]
    dpeers = [lax.rem(di + o, parts) for o in range(1, parts)]
    xpeers = [lax.rem(x + o, nx) for o in range(1, nx)]
    zpeers = [lax.rem(z + o, nz) for o in range(1, nz)]

    barrier = pltpu.get_barrier_semaphore()
    everyone = [mate] + ypeers + [(fi, p) for p in dpeers]
    for device in everyone:
        pl.semaphore_signal(barrier, inc=1, device_id=device, device_id_type=pl.DeviceIdType.MESH)

    flat = feats[...].reshape(feat * n, cols)

    def project(h):
        for t in range(w // TILE):
            acc = dot(flat, w_one[:, h * w + t * TILE : h * w + (t + 1) * TILE])
            for f in range(feat):
                part = acc[f * n : (f + 1) * n]
                rows = slice((f // 2) * n, (f // 2 + 1) * n)
                lanes = slice(t * TILE, (t + 1) * TILE)
                proj[h, f % 2, rows, lanes] = part
                projb[h, f % 2, rows, lanes] = part.astype(BF)

    def core_send(h):
        return send(projb.at[h, 1 - c], r1.at[h], mate)

    def y_send(h):
        for j in range(ny):
            rows = slice(j * n, (j + 1) * n)
            qb[h, j] = (proj[h, c, rows] + r1[h, rows].astype(F32)).astype(BF)
        mine = pl.ds(pl.multiple_of(y * n, n), n)
        q[h] = proj[h, c, mine] + r1[h, mine].astype(F32)
        return [
            send(qb.at[h, lax.rem(y + o, ny)], r2.at[h, o - 1], ypeers[o - 1])
            for o in range(1, ny)
        ]

    def owned(h):
        total = q[h]
        for o in range(ny - 1):
            total = total + r2[h, o].astype(F32)
        return total

    def wait(items):
        for item in items:
            item.wait_recv()

    def slot(p):
        return pl.ds(pl.multiple_of(p * SLOT, SLOT), SLOT)

    def table_slot(p):
        return pl.ds(pl.multiple_of(n + p * SLOT, SLOT), SLOT)

    def trade_rows(values, boxes, table):
        table[:n] = values
        boxes[...] = dot(sm[...], values).astype(BF)
        table[table_slot(di)] = boxes[slot(di)]
        return [send(boxes.at[slot(p)], table.at[table_slot(di)], (fi, p)) for p in dpeers]

    def trade_back(values, outgoing, returned):
        terms = dot(ct[...], (values * inv[...]).astype(BF))
        outgoing[...] = terms[n:].astype(BF)
        returned[slot(di)] = outgoing[slot(di)]
        moves = [send(outgoing.at[slot(p)], returned.at[slot(di)], (fi, p)) for p in dpeers]
        return terms[:n], moves

    def gather_start(h):
        block = dp.at[fi, :, h * w : (h + 1) * w]
        return [send(block, block, device) for device in ypeers], send(block, block, mate)

    def gather_forward(h, moves):
        across = []
        for o in range(1, ny):
            moves[o - 1].wait_recv()
            source = lax.rem(y - o + ny, ny) * 2 + c
            block = dp.at[source, :, h * w : (h + 1) * w]
            across.append(send(block, block, mate))
        return across

    project(1)
    pl.semaphore_wait(barrier, len(everyone))
    near_core = core_send(1)
    project(0)
    self_core = core_send(0)
    near_core.wait_recv()
    near_y = y_send(1)
    self_core.wait_recv()
    self_y = y_send(0)

    col = lax.broadcasted_iota(jnp.int32, (n, n + parts * SLOT), 1)
    extra = col - n
    code = jnp.where(
        col < n, col, jnp.where(extra % SLOT < kmax, n + (extra // SLOT) * kmax + extra % SLOT, -2)
    )
    counts = jnp.zeros(code.shape, F32)
    for s in range(fan):
        counts = counts + jnp.where(nbr[:, s : s + 1] == code, 1.0, 0.0)
    cm[...] = counts.astype(BF)
    ct[...] = counts.T.astype(BF)
    picks = jnp.where(
        sidx[...] == lax.broadcasted_iota(jnp.int32, (parts * SLOT, n), 1), 1.0, 0.0
    )
    sm[...] = picks.astype(BF)
    st[...] = picks.T.astype(BF)
    dcat = dot_nt(grads[...], w_two[...])
    dcs[...] = dcat[:, :w]
    local, back_agg = trade_back(dcat[:, w:], k0, h0)
    dcs[...] += local
    ft[...] = flat.T

    wait(near_y)
    rows_near = trade_rows(owned(1).astype(BF), b1, t1)
    wait(self_y)
    pself[...] = owned(0)
    wait(back_agg)
    dh[...] = dcs[...] + dot(st[...], h0[...])
    wait(rows_near)
    pre = pself[...] + dot(cm[...], t1[...]) * inv[...]
    sig = 1.0 / (1.0 + jnp.exp(-pre))
    d_pre = dh[...] * sig * (1.0 + pre * (1.0 - sig))
    dp[fi, :, :w] = d_pre.astype(BF)
    near_local, back_pre = trade_back(d_pre, k1, h1)
    dnl[...] = near_local
    gather0, across0 = gather_start(0)
    hidden = (pre * sig).astype(BF)
    joined[:, :w] = hidden
    rows_hidden = trade_rows(hidden, b2, t2)

    wait(back_pre)
    dp[fi, :, w:] = (dnl[...] + dot(st[...], h1[...])).astype(BF)
    gather1, across1 = gather_start(1)
    forward0 = gather_forward(0, gather0)

    wait(rows_hidden)
    agg = dot(cm[...], t2[...]) * inv[...]
    joined[:, w:] = agg.astype(BF)
    both = joined[...]
    out[0] = dot(both, w_two[...]).astype(BF)
    span = two.shape[0] // feat
    two_part = dot(both.T, grads[...]).astype(BF)
    for f in range(feat):
        ts[f % 2, (f // 2) * span : (f // 2 + 1) * span] = two_part[f * span : (f + 1) * span]
    two_core = send(ts.at[1 - c], u1, mate)

    forward1 = gather_forward(1, gather1)

    rows_x = cols // nx
    rows_z = rows_x // nz

    def lanes_of(k):
        return slice(k * TILE, (k + 1) * TILE)

    def chunk(k):
        lanes = lanes_of(k)
        g[:, lanes] = dot(ft[...], dp[:, :, lanes].reshape(feat * n, TILE)).astype(BF)
        return [
            send(g.at[pl.ds(pl.multiple_of(t * rows_x, SLOT), rows_x), lanes],
                 rx.at[o, :, lanes], (fi, z * nx + t))
            for o, t in enumerate(xpeers)
        ]

    def z_scatter(k, moves):
        wait(moves)
        lanes = lanes_of(k)
        total = g[pl.ds(pl.multiple_of(x * rows_x, SLOT), rows_x), lanes].astype(F32)
        for o in range(nx - 1):
            total = total + rx[o, :, lanes].astype(F32)
        sx[:, lanes] = total.astype(BF)
        return [
            send(sx.at[pl.ds(pl.multiple_of(t * rows_z, SLOT), rows_z), lanes],
                 rz.at[o, :, lanes], (fi, t * nx + x))
            for o, t in enumerate(zpeers)
        ]

    def z_gather(k, moves):
        wait(moves)
        lanes = lanes_of(k)
        total = sx[pl.ds(pl.multiple_of(z * rows_z, SLOT), rows_z), lanes].astype(F32)
        for o in range(nz - 1):
            total = total + rz[o, :, lanes].astype(F32)
        mine = pl.ds(pl.multiple_of(x * rows_x + z * rows_z, SLOT), rows_z)
        one[mine, lanes] = total.astype(BF)
        piece = one.at[mine, lanes]
        return [send(piece, piece, (fi, t * nx + x)) for t in zpeers]

    def x_gather(k, moves):
        wait(moves)
        piece = one.at[pl.ds(pl.multiple_of(x * rows_x, SLOT), rows_x), lanes_of(k)]
        return [send(piece, piece, (fi, z * nx + t)) for t in xpeers]

    lanes_x = w // nx
    span_z = span // nz
    my_lanes = pl.ds(pl.multiple_of(x * lanes_x, 128), lanes_x)

    def two_y():
        two_core.wait_recv()
        ub[...] = (ts[c].astype(F32) + u1[...].astype(F32)).astype(BF)
        return [
            send(ub.at[pl.ds(pl.multiple_of(lax.rem(y + o, ny) * span, SLOT), span)],
                 u2.at[o - 1], ypeers[o - 1])
            for o in range(1, ny)
        ]

    def two_x(moves):
        wait(moves)
        total = ub[pl.ds(pl.multiple_of(y * span, SLOT), span)].astype(F32)
        for o in range(ny - 1):
            total = total + u2[o].astype(F32)
        for t in range(nx):
            v[t] = total[:, t * lanes_x : (t + 1) * lanes_x].astype(BF)
        return [send(v.at[t], vx.at[o], (fi, z * nx + t)) for o, t in enumerate(xpeers)]

    def two_z(moves):
        wait(moves)
        total = v[x].astype(F32)
        for o in range(nx - 1):
            total = total + vx[o].astype(F32)
        vs[...] = total.astype(BF)
        return [
            send(vs.at[pl.ds(pl.multiple_of(t * span_z, SLOT), span_z)], vz.at[o], (fi, t * nx + x))
            for o, t in enumerate(zpeers)
        ]

    def two_zg(moves):
        wait(moves)
        total = vs[pl.ds(pl.multiple_of(z * span_z, SLOT), span_z)].astype(F32)
        for o in range(nz - 1):
            total = total + vz[o].astype(F32)
        mine = pl.ds(pl.multiple_of(fi * span + z * span_z, SLOT), span_z)
        two[mine, my_lanes] = total.astype(BF)
        piece = two.at[mine, my_lanes]
        return [send(piece, piece, (fi, t * nx + x)) for t in zpeers]

    def two_xg(moves):
        wait(moves)
        piece = two.at[pl.ds(pl.multiple_of(fi * span, SLOT), span), my_lanes]
        return [send(piece, piece, (fi, z * nx + t)) for t in xpeers]

    def two_yg(moves):
        wait(moves)
        piece = two.at[pl.ds(pl.multiple_of(fi * span, SLOT), span)]
        return [send(piece, piece, device) for device in ypeers], send(piece, piece, mate)

    def two_across(moves):
        across = []
        for o in range(1, ny):
            moves[o - 1].wait_recv()
            source = lax.rem(y - o + ny, ny) * 2 + c
            piece = two.at[pl.ds(pl.multiple_of(source * span, SLOT), span)]
            across.append(send(piece, piece, mate))
        return across

    chunks = 2 * w // TILE
    half = chunks // 2
    moves = {}
    two_moves = two_y()
    across0.wait_recv()
    wait(forward0)
    for k in range(half):
        moves[k] = chunk(k)
    two_moves = two_x(two_moves)
    across1.wait_recv()
    wait(forward1)
    for k in range(half, chunks):
        moves[k] = chunk(k)
    stages = [z_scatter, z_gather, x_gather]
    two_stages = [two_z, two_zg, two_xg]
    for step in range(chunks + len(stages) - 1):
        for s in reversed(range(len(stages))):
            k = step - s
            if 0 <= k < chunks:
                moves[k] = stages[s](k, moves[k])
        if step < len(two_stages):
            two_moves = two_stages[step](two_moves)
        elif step == len(two_stages):
            two_moves, two_mate = two_yg(two_moves)
        elif step == len(two_stages) + 1:
            two_moves = two_across(two_moves)
    for k in range(chunks):
        wait(moves[k])
    wait(two_moves)
    two_mate.wait_recv()
    for copy in copies:
        copy.wait_send()


def on_device(nx, nz, features, w_one, w_two, neighbor, degree, send_rows, grad_out):
    feat, n, cols = features.shape
    w = w_two.shape[1]
    ny = feat // 2
    parts, kmax = send_rows.shape[1:]
    fan = neighbor.shape[2]
    slots = jnp.arange(fan, dtype=jnp.int32)
    nbr = jnp.where(slots[None, :] < degree[0][:, None], neighbor[0], -1)
    inv = 1.0 / degree[0].astype(F32)[:, None]
    sidx = jnp.pad(send_rows[0], ((0, 0), (0, SLOT - kmax)), constant_values=-1).reshape(-1, 1)
    table = n + parts * SLOT
    edge = parts * SLOT
    rows_x = cols // nx
    rows_z = rows_x // nz
    span = 2 * w // feat
    lanes_x = w // nx
    chunks = 2 * w // TILE
    n_copies = (
        2 + 4 * (ny - 1) + 4 * (parts - 1) + 2 + 2 * (ny - 1)
        + chunks * 2 * (nx - 1 + nz - 1)
        + 1 + (ny - 1) + 2 * (nx - 1 + nz - 1) + 2 * (ny - 1) + 1
    )
    vm = pltpu.VMEM
    scratch = [
        vm((2, 2, ny * n, w), F32), vm((2, 2, ny * n, w), BF), vm((2, ny * n, w), BF),
        vm((2, n, w), F32), vm((2, ny, n, w), BF), vm((2, ny - 1, n, w), BF),
        vm((n, table), BF), vm((table, n), BF), vm((edge, n), BF), vm((n, edge), BF),
        vm((table, w), BF), vm((table, w), BF), vm((edge, w), BF), vm((edge, w), BF),
        vm((edge, w), BF), vm((edge, w), BF), vm((edge, w), BF), vm((edge, w), BF),
        vm((n, w), F32), vm((n, w), F32), vm((n, w), F32), vm((n, w), F32),
        vm((n, 2 * w), BF), vm((cols, feat * n), BF), vm((feat, n, 2 * w), BF),
        vm((cols, 2 * w), BF), vm((nx - 1, rows_x, 2 * w), BF), vm((rows_x, 2 * w), BF),
        vm((nz - 1, rows_z, 2 * w), BF),
        vm((2, ny * span, w), BF), vm((ny * span, w), BF), vm((ny * span, w), BF),
        vm((ny - 1, span, w), BF), vm((nx, span, lanes_x), BF), vm((nx - 1, span, lanes_x), BF),
        vm((span, lanes_x), BF), vm((nz - 1, span // nz, lanes_x), BF),
        pltpu.SemaphoreType.DMA((n_copies,)), pltpu.SemaphoreType.DMA((n_copies,)),
    ]
    spec = pl.BlockSpec(memory_space=pltpu.VMEM)
    out, one_sum, two_sum = pl.pallas_call(
        functools.partial(kernel, feat, nx, nz, kmax),
        out_shape=(
            jax.ShapeDtypeStruct((1, n, w), BF),
            jax.ShapeDtypeStruct((cols, 2 * w), BF),
            jax.ShapeDtypeStruct((2 * w, w), BF),
        ),
        in_specs=[spec] * 7,
        out_specs=(spec, spec, spec),
        scratch_shapes=scratch,
        compiler_params=pltpu.CompilerParams(
            collective_id=0, has_side_effects=True, vmem_limit_bytes=56 * 1024 * 1024
        ),
    )(features, w_one, w_two, nbr, inv, sidx, grad_out[0])
    scale = 1.0 / math.sqrt(feat * n * parts)
    return out, one_sum.astype(F32) * scale, two_sum.astype(F32) * scale


def solution(mesh):
    parts = mesh.shape["dom"]
    nx = 1 << ((parts.bit_length() - 2) // 2)
    in_specs = (
        P(None, "dom", "feat"),
        P("feat", None),
        P(),
        P("feat", "dom", None),
        P("feat", "dom"),
        P("feat", "dom", None),
        P("feat", "dom", None),
    )
    out_specs = (P("feat", "dom", None), P("feat", None), P())
    return jax.shard_map(
        functools.partial(on_device, nx, parts // nx),
        mesh=mesh, in_specs=in_specs, out_specs=out_specs, check_vma=False,
    )
```

```python
import functools
import math

import jax
import jax.numpy as jnp
from jax import lax
from jax.experimental import pallas as pl
from jax.experimental.pallas import tpu as pltpu
from jax.sharding import PartitionSpec as P

BF = jnp.bfloat16
F32 = jnp.float32
SLOT = 16
TILE = 256


def dot(a, b):
    return jnp.dot(a, b, preferred_element_type=F32)


def dot_nt(a, b):
    return lax.dot_general(a, b, (((1,), (1,)), ((), ())), preferred_element_type=F32)


def kernel(
    feat, nx, nz, kmax,
    feats, w_one, w_two, nbr, deg, sends, grads,
    out, one, two,
    proj, projb, r1, q, qb, r2, cm, ct, sm, st, t1, t2, b1, b2, k0, k1, h0, h1,
    inv, dcs, dh, pself, dnl, joined, fx, ft, dp, g, rx, sx, rz, ts, u1, ub, u2, v, vx, vs, vz,
    ssem, rsem,
):
    ny = feat // 2
    parts = nx * nz
    n = nbr.shape[1]
    w = grads.shape[1]
    cols = w_one.shape[0]
    fan = nbr.shape[0]
    half_cols = cols // 2
    fi = lax.axis_index("feat")
    di = lax.axis_index("dom")
    y, c = fi // 2, fi % 2
    z, x = di // nx, di % nx
    mate = (y * 2 + 1 - c, di)
    zlow, zhigh = z % 2, z // 2
    pair = (fi, (z + 1 - 2 * zlow) * nx + x)
    count = [0]

    def send(src, dst, device):
        k = count[0]
        count[0] += 1
        copy = pltpu.make_async_remote_copy(
            src_ref=src, dst_ref=dst, send_sem=ssem.at[k], recv_sem=rsem.at[k],
            device_id=device, device_id_type=pl.DeviceIdType.MESH,
        )
        copy.start()
        copies.append(copy)
        return copy

    copies = []
    ypeers = [(lax.rem(y + o, ny) * 2 + c, di) for o in range(1, ny)]
    dpeers = [lax.rem(di + o, parts) for o in range(1, parts)]
    xpeers = [lax.rem(x + o, nx) for o in range(1, nx)]
    zpeers = [lax.rem(zhigh + o, nz // 2) * 2 + zlow for o in range(1, nz // 2)]

    barrier = pltpu.get_barrier_semaphore()
    everyone = [mate] + ypeers + [(fi, p) for p in dpeers]
    for device in everyone:
        pl.semaphore_signal(barrier, inc=1, device_id=device, device_id_type=pl.DeviceIdType.MESH)

    flat = feats[...].reshape(feat * n, cols)

    def project(h):
        for t in range(w // TILE):
            acc = dot(flat, w_one[:, h * w + t * TILE : h * w + (t + 1) * TILE])
            for f in range(feat):
                part = acc[f * n : (f + 1) * n]
                rows = slice((f // 2) * n, (f // 2 + 1) * n)
                lanes = slice(t * TILE, (t + 1) * TILE)
                proj[h, f % 2, rows, lanes] = part
                projb[h, f % 2, rows, lanes] = part.astype(BF)

    def core_send(h):
        return send(projb.at[h, 1 - c], r1.at[h], mate)

    def y_send(h):
        for j in range(ny):
            rows = slice(j * n, (j + 1) * n)
            qb[h, j] = (proj[h, c, rows] + r1[h, rows].astype(F32)).astype(BF)
        mine = pl.ds(pl.multiple_of(y * n, n), n)
        q[h] = proj[h, c, mine] + r1[h, mine].astype(F32)
        return [
            send(qb.at[h, lax.rem(y + o, ny)], r2.at[h, o - 1], ypeers[o - 1])
            for o in range(1, ny)
        ]

    def owned(h):
        total = q[h]
        for o in range(ny - 1):
            total = total + r2[h, o].astype(F32)
        return total

    def wait(items):
        for item in items:
            item.wait_recv()

    def slot(p):
        return pl.ds(pl.multiple_of(p * SLOT, SLOT), SLOT)

    def table_slot(p):
        return pl.ds(pl.multiple_of(n + p * SLOT, SLOT), SLOT)

    def trade_rows(values, boxes, table):
        table[:n] = values
        boxes[...] = dot(sm[...], values).astype(BF)
        table[table_slot(di)] = boxes[slot(di)]
        return [send(boxes.at[slot(p)], table.at[table_slot(di)], (fi, p)) for p in dpeers]

    def trade_back(values, outgoing, returned):
        terms = dot(ct[...], (values * inv[...]).astype(BF))
        outgoing[...] = terms[n:].astype(BF)
        returned[slot(di)] = outgoing[slot(di)]
        moves = [send(outgoing.at[slot(p)], returned.at[slot(di)], (fi, p)) for p in dpeers]
        return terms[:n], moves

    def block(low, f, h):
        return dp.at[low, f, :, h * w : (h + 1) * w]

    def pass_on(low, f, h, device):
        return send(block(low, f, h), block(low, f, h), device)

    def y_source(o):
        return lax.rem(y - o + ny, ny) * 2 + c

    def gather_start(h):
        to_pair = pass_on(zlow, fi, h, pair)
        to_y = [pass_on(zlow, fi, h, device) for device in ypeers]
        return to_pair, to_y, [pass_on(zlow, fi, h, mate)]

    def gather_y_first(h, to_pair, to_y, to_mate):
        paired = [to_pair]
        for o in range(1, ny):
            to_y[o - 1].wait_recv()
            paired.append(pass_on(zlow, y_source(o), h, pair))
            to_mate.append(pass_on(zlow, y_source(o), h, mate))
        for o in range(ny):
            paired[o].wait_recv()
            to_mate.append(pass_on(1 - zlow, y_source(o), h, mate))
        return to_mate

    def gather_pair_first(h, to_pair, to_y, to_mate):
        to_pair.wait_recv()
        far = [pass_on(1 - zlow, fi, h, device) for device in ypeers]
        to_mate.append(pass_on(1 - zlow, fi, h, mate))
        for low, moves in ((zlow, to_y), (1 - zlow, far)):
            for o in range(1, ny):
                moves[o - 1].wait_recv()
                to_mate.append(pass_on(low, y_source(o), h, mate))
        return to_mate

    project(1)
    pl.semaphore_wait(barrier, len(everyone))
    near_core = core_send(1)
    far_cols = pl.ds(pl.multiple_of((1 - zlow) * half_cols, 128), half_cols)
    near_cols = pl.ds(pl.multiple_of(zlow * half_cols, 128), half_cols)
    features_move = send(feats.at[:, :, far_cols], fx, pair)
    project(0)
    self_core = core_send(0)
    near_core.wait_recv()
    near_y = y_send(1)
    self_core.wait_recv()
    self_y = y_send(0)

    eye = lax.broadcasted_iota(jnp.int32, (n, n), 0) == lax.broadcasted_iota(jnp.int32, (n, n), 1)
    inv[...] = 1.0 / jnp.sum(jnp.where(eye, deg[...].astype(F32), 0.0), axis=1, keepdims=True)
    entry = lax.broadcasted_iota(jnp.int32, (n + parts * SLOT, n), 0)
    extra = entry - n
    code = jnp.where(
        entry < n, entry,
        jnp.where(extra % SLOT < kmax, n + (extra // SLOT) * kmax + extra % SLOT, -2),
    )
    counts = jnp.zeros(code.shape, F32)
    for s in range(fan):
        used = jnp.where(s < deg[...], nbr[s : s + 1], -1)
        counts = counts + jnp.where(used == code, 1.0, 0.0)
    ct[...] = counts.astype(BF)
    cm[...] = counts.T.astype(BF)
    edge = (parts * SLOT, parts)
    owner = lax.broadcasted_iota(jnp.int32, edge, 0) // SLOT == lax.broadcasted_iota(jnp.int32, edge, 1)
    spread_rows = dot(jnp.where(owner, 1.0, 0.0).astype(BF), sends[...].astype(F32).astype(BF))
    place = (parts * SLOT, kmax)
    here = lax.broadcasted_iota(jnp.int32, place, 0) % SLOT == lax.broadcasted_iota(jnp.int32, place, 1)
    chosen = jnp.sum(jnp.where(here, spread_rows + 1.0, 0.0), axis=1, keepdims=True) - 1.0
    lane = lax.broadcasted_iota(jnp.int32, (parts * SLOT, n), 1).astype(F32)
    picks = jnp.where(chosen == lane, 1.0, 0.0)
    sm[...] = picks.astype(BF)
    st[...] = picks.T.astype(BF)
    dcat = dot_nt(grads[...], w_two[...])
    dcs[...] = dcat[:, :w]
    local, back_agg = trade_back(dcat[:, w:], k0, h0)
    dcs[...] += local
    ft[zlow] = feats[:, :, near_cols].reshape(feat * n, half_cols).T

    wait(near_y)
    rows_near = trade_rows(owned(1).astype(BF), b1, t1)
    wait(self_y)
    pself[...] = owned(0)
    wait(back_agg)
    dh[...] = dcs[...] + dot(st[...], h0[...])
    wait(rows_near)
    pre = pself[...] + dot(cm[...], t1[...]) * inv[...]
    sig = 1.0 / (1.0 + jnp.exp(-pre))
    d_pre = dh[...] * sig * (1.0 + pre * (1.0 - sig))
    dp[zlow, fi, :, :w] = d_pre.astype(BF)
    near_local, back_pre = trade_back(d_pre, k1, h1)
    dnl[...] = near_local
    gather0 = gather_start(0)
    hidden = (pre * sig).astype(BF)
    joined[:, :w] = hidden
    rows_hidden = trade_rows(hidden, b2, t2)

    wait(back_pre)
    dp[zlow, fi, :, w:] = (dnl[...] + dot(st[...], h1[...])).astype(BF)
    gather1 = gather_start(1)
    features_move.wait_recv()
    ft[1 - zlow] = fx[...].reshape(feat * n, half_cols).T

    wait(rows_hidden)
    agg = dot(cm[...], t2[...]) * inv[...]
    joined[:, w:] = agg.astype(BF)
    both = joined[...]
    out[0] = dot(both, w_two[...]).astype(BF)
    span = two.shape[0] // feat
    two_part = dot(both.T, grads[...]).astype(BF)
    for f in range(feat):
        ts[f % 2, (f // 2) * span : (f // 2 + 1) * span] = two_part[f * span : (f + 1) * span]
    two_core = send(ts.at[1 - c], u1, mate)

    arrived0 = gather_y_first(0, *gather0)
    arrived1 = gather_pair_first(1, *gather1)

    rows_x = half_cols // nx
    rows_z = rows_x // (nz // 2)

    def lanes_of(k):
        return slice(k * TILE, (k + 1) * TILE)

    def chunk(k):
        lanes = lanes_of(k)
        g[:, lanes] = (
            dot(ft[0], dp[0, :, :, lanes].reshape(feat * n, TILE))
            + dot(ft[1], dp[1, :, :, lanes].reshape(feat * n, TILE))
        ).astype(BF)
        return [
            send(g.at[pl.ds(pl.multiple_of(t * rows_x, SLOT), rows_x), lanes],
                 rx.at[o, :, lanes], (fi, z * nx + t))
            for o, t in enumerate(xpeers)
        ]

    def z_scatter(k, moves):
        wait(moves)
        lanes = lanes_of(k)
        total = g[pl.ds(pl.multiple_of(x * rows_x, SLOT), rows_x), lanes].astype(F32)
        for o in range(nx - 1):
            total = total + rx[o, :, lanes].astype(F32)
        sx[:, lanes] = total.astype(BF)
        return [
            send(sx.at[pl.ds(pl.multiple_of((t // 2) * rows_z, SLOT), rows_z), lanes],
                 rz.at[o, :, lanes], (fi, t * nx + x))
            for o, t in enumerate(zpeers)
        ]

    def piece(k, low, at):
        return one.at[pl.ds(pl.multiple_of(low * half_cols + at * rows_x, SLOT), rows_x), lanes_of(k)]

    def z_gather(k, moves):
        wait(moves)
        lanes = lanes_of(k)
        total = sx[pl.ds(pl.multiple_of(zhigh * rows_z, SLOT), rows_z), lanes].astype(F32)
        for o in range(nz // 2 - 1):
            total = total + rz[o, :, lanes].astype(F32)
        mine = pl.ds(
            pl.multiple_of(zlow * half_cols + x * rows_x + zhigh * rows_z, SLOT), rows_z
        )
        one[mine, lanes] = total.astype(BF)
        return [send(one.at[mine, lanes], one.at[mine, lanes], (fi, t * nx + x)) for t in zpeers]

    def first_gather(k, moves):
        wait(moves)
        mine = piece(k, zlow, x)
        to_x = [send(mine, mine, (fi, z * nx + t)) for t in xpeers]
        return to_x, send(mine, mine, pair)

    def last_gather(k, moves):
        to_x, to_pair = moves
        rest = []
        if k % 2:
            to_pair.wait_recv()
            got = piece(k, 1 - zlow, x)
            rest = [send(got, got, (fi, z * nx + t)) for t in xpeers]
            return to_x + rest
        for o in range(1, nx):
            to_x[o - 1].wait_recv()
            got = piece(k, zlow, lax.rem(x - o + nx, nx))
            rest.append(send(got, got, pair))
        return [to_pair] + rest

    lanes_x = w // nx
    span_z = span // nz
    allz = [lax.rem(z + o, nz) for o in range(1, nz)]
    my_lanes = pl.ds(pl.multiple_of(x * lanes_x, 128), lanes_x)

    def two_y():
        two_core.wait_recv()
        ub[...] = (ts[c].astype(F32) + u1[...].astype(F32)).astype(BF)
        return [
            send(ub.at[pl.ds(pl.multiple_of(lax.rem(y + o, ny) * span, SLOT), span)],
                 u2.at[o - 1], ypeers[o - 1])
            for o in range(1, ny)
        ]

    def two_x(moves):
        wait(moves)
        total = ub[pl.ds(pl.multiple_of(y * span, SLOT), span)].astype(F32)
        for o in range(ny - 1):
            total = total + u2[o].astype(F32)
        for t in range(nx):
            v[t] = total[:, t * lanes_x : (t + 1) * lanes_x].astype(BF)
        return [send(v.at[t], vx.at[o], (fi, z * nx + t)) for o, t in enumerate(xpeers)]

    def two_z(moves):
        wait(moves)
        total = v[x].astype(F32)
        for o in range(nx - 1):
            total = total + vx[o].astype(F32)
        vs[...] = total.astype(BF)
        return [
            send(vs.at[pl.ds(pl.multiple_of(t * span_z, SLOT), span_z)], vz.at[o], (fi, t * nx + x))
            for o, t in enumerate(allz)
        ]

    def two_zg(moves):
        wait(moves)
        total = vs[pl.ds(pl.multiple_of(z * span_z, SLOT), span_z)].astype(F32)
        for o in range(nz - 1):
            total = total + vz[o].astype(F32)
        mine = pl.ds(pl.multiple_of(fi * span + z * span_z, SLOT), span_z)
        two[mine, my_lanes] = total.astype(BF)
        piece = two.at[mine, my_lanes]
        return [send(piece, piece, (fi, t * nx + x)) for t in allz]

    def two_xg(moves):
        wait(moves)
        piece = two.at[pl.ds(pl.multiple_of(fi * span, SLOT), span), my_lanes]
        return [send(piece, piece, (fi, z * nx + t)) for t in xpeers]

    def two_yg(moves):
        wait(moves)
        piece = two.at[pl.ds(pl.multiple_of(fi * span, SLOT), span)]
        return [send(piece, piece, device) for device in ypeers], send(piece, piece, mate)

    def two_across(moves):
        across = []
        for o in range(1, ny):
            moves[o - 1].wait_recv()
            source = lax.rem(y - o + ny, ny) * 2 + c
            piece = two.at[pl.ds(pl.multiple_of(source * span, SLOT), span)]
            across.append(send(piece, piece, mate))
        return across

    chunks = 2 * w // TILE
    half = chunks // 2
    moves = {}
    two_moves = two_y()
    wait(arrived0)
    for k in range(half):
        moves[k] = chunk(k)
    two_moves = two_x(two_moves)
    wait(arrived1)
    for k in range(half, chunks):
        moves[k] = chunk(k)
    stages = [z_scatter, z_gather, first_gather, last_gather]
    two_stages = [two_z, two_zg, two_xg]
    for step in range(chunks + len(stages) - 1):
        for s in reversed(range(len(stages))):
            k = step - s
            if 0 <= k < chunks:
                moves[k] = stages[s](k, moves[k])
        if step < len(two_stages):
            two_moves = two_stages[step](two_moves)
        elif step == len(two_stages):
            two_moves, two_mate = two_yg(two_moves)
        elif step == len(two_stages) + 1:
            two_moves = two_across(two_moves)
    for k in range(chunks):
        wait(moves[k])
    wait(two_moves)
    two_mate.wait_recv()
    for copy in copies:
        copy.wait_send()


def on_device(nx, nz, features, w_one, w_two, neighbor, degree, send_rows, grad_out):
    feat, n, cols = features.shape
    w = w_two.shape[1]
    ny = feat // 2
    parts, kmax = send_rows.shape[1:]
    table = n + parts * SLOT
    edge = parts * SLOT
    half_cols = cols // 2
    rows_x = half_cols // nx
    rows_z = rows_x // (nz // 2)
    span = 2 * w // feat
    lanes_x = w // nx
    chunks = 2 * w // TILE
    n_copies = (
        3 + 2 * (ny - 1) + 4 * (parts - 1) + 2 * (2 + 2 * ny) + 4 * ny
        + chunks * (4 * nx + nz)
        + 2 + 4 * ny + 2 * (nx + nz)
    )
    vm = pltpu.VMEM
    scratch = [
        vm((2, 2, ny * n, w), F32), vm((2, 2, ny * n, w), BF), vm((2, ny * n, w), BF),
        vm((2, n, w), F32), vm((2, ny, n, w), BF), vm((2, ny - 1, n, w), BF),
        vm((n, table), BF), vm((table, n), BF), vm((edge, n), BF), vm((n, edge), BF),
        vm((table, w), BF), vm((table, w), BF), vm((edge, w), BF), vm((edge, w), BF),
        vm((edge, w), BF), vm((edge, w), BF), vm((edge, w), BF), vm((edge, w), BF),
        vm((n, 1), F32), vm((n, w), F32), vm((n, w), F32), vm((n, w), F32), vm((n, w), F32),
        vm((n, 2 * w), BF), vm((feat, n, half_cols), BF), vm((2, half_cols, feat * n), BF),
        vm((2, feat, n, 2 * w), BF),
        vm((half_cols, 2 * w), BF), vm((nx - 1, rows_x, 2 * w), BF), vm((rows_x, 2 * w), BF),
        vm((nz // 2 - 1, rows_z, 2 * w), BF),
        vm((2, ny * span, w), BF), vm((ny * span, w), BF), vm((ny * span, w), BF),
        vm((ny - 1, span, w), BF), vm((nx, span, lanes_x), BF), vm((nx - 1, span, lanes_x), BF),
        vm((span, lanes_x), BF), vm((nz - 1, span // nz, lanes_x), BF),
        pltpu.SemaphoreType.DMA((n_copies,)), pltpu.SemaphoreType.DMA((n_copies,)),
    ]
    spec = pl.BlockSpec(memory_space=pltpu.VMEM)
    out, one_sum, two_sum = pl.pallas_call(
        functools.partial(kernel, feat, nx, nz, kmax),
        out_shape=(
            jax.ShapeDtypeStruct((1, n, w), BF),
            jax.ShapeDtypeStruct((cols, 2 * w), BF),
            jax.ShapeDtypeStruct((2 * w, w), BF),
        ),
        in_specs=[spec] * 7,
        out_specs=(spec, spec, spec),
        scratch_shapes=scratch,
        compiler_params=pltpu.CompilerParams(
            collective_id=0, has_side_effects=True, vmem_limit_bytes=40 * 1024 * 1024
        ),
    )(features, w_one, w_two, neighbor[0].T, degree, send_rows[0], grad_out[0])
    scale = 1.0 / math.sqrt(feat * n * parts)
    return out, one_sum.astype(F32) * scale, two_sum.astype(F32) * scale


def solution(mesh):
    parts = mesh.shape["dom"]
    nx = 1 << ((parts.bit_length() - 2) // 2)
    in_specs = (
        P(None, "dom", "feat"),
        P("feat", None),
        P(),
        P("feat", "dom", None),
        P("feat", "dom"),
        P("feat", "dom", None),
        P("feat", "dom", None),
    )
    out_specs = (P("feat", "dom", None), P("feat", None), P())
    return jax.shard_map(
        functools.partial(on_device, nx, parts // nx),
        mesh=mesh, in_specs=in_specs, out_specs=out_specs, check_vma=False,
    )
```

```python
import functools
import math

import jax
import jax.numpy as jnp
from jax import lax
from jax.experimental import pallas as pl
from jax.experimental.pallas import tpu as pltpu
from jax.sharding import PartitionSpec as P

BF = jnp.bfloat16
F32 = jnp.float32
SLOT = 16
TILE = 256


def dot(a, b):
    return jnp.dot(a, b, preferred_element_type=F32)


def dot_nt(a, b):
    return lax.dot_general(a, b, (((1,), (1,)), ((), ())), preferred_element_type=F32)


def kernel(
    feat, nx, nz, kmax,
    feats_hbm, w_one_hbm, w_two_hbm, nbr_hbm, deg_hbm, sends_hbm, grads_hbm,
    out, one, two,
    feats, w_one, w_two, nbr, deg, sends, grads,
    proj, projb, r1, q, qb, r2, cm, ct, sm, st, t1, t2, b1, b2, k0, k1, h0, h1,
    inv, dcs, dh, pself, dnl, joined, fx, ft, dp, g, rx, sx, rz, ts, u1, ub, u2, v, vx, vs, vz,
    ssem, rsem, lsem,
):
    ny = feat // 2
    parts = nx * nz
    n = nbr.shape[2]
    w = grads.shape[1]
    cols = w_one.shape[0]
    fan = nbr.shape[0]
    half_cols = cols // 2
    fi = lax.axis_index("feat")
    di = lax.axis_index("dom")
    y, c = fi // 2, fi % 2
    z, x = di // nx, di % nx
    mate = (y * 2 + 1 - c, di)
    zlow, zhigh = z % 2, z // 2
    pair = (fi, (z + 1 - 2 * zlow) * nx + x)
    count = [0]

    def send(src, dst, device):
        k = count[0]
        count[0] += 1
        copy = pltpu.make_async_remote_copy(
            src_ref=src, dst_ref=dst, send_sem=ssem.at[k], recv_sem=rsem.at[k],
            device_id=device, device_id_type=pl.DeviceIdType.MESH,
        )
        copy.start()
        copies.append(copy)
        return copy

    copies = []
    ypeers = [(lax.rem(y + o, ny) * 2 + c, di) for o in range(1, ny)]
    dpeers = [lax.rem(di + o, parts) for o in range(1, parts)]
    xpeers = [lax.rem(x + o, nx) for o in range(1, nx)]
    zpeers = [lax.rem(zhigh + o, nz // 2) * 2 + zlow for o in range(1, nz // 2)]

    barrier = pltpu.get_barrier_semaphore()
    everyone = [mate] + ypeers + [(fi, p) for p in dpeers]
    for device in everyone:
        pl.semaphore_signal(barrier, inc=1, device_id=device, device_id_type=pl.DeviceIdType.MESH)

    def load(k, src, dst):
        copy = pltpu.make_async_copy(src, dst, lsem.at[k])
        copy.start()
        return copy

    first_loads = [load(0, w_one_hbm.at[:, w:], w_one.at[:, w:]), load(1, feats_hbm, feats)]
    self_load = load(2, w_one_hbm.at[:, :w], w_one.at[:, :w])
    later_loads = [
        load(3, nbr_hbm, nbr), load(4, deg_hbm, deg), load(5, sends_hbm, sends),
        load(6, grads_hbm, grads), load(7, w_two_hbm, w_two),
    ]

    def project(h):
        flat = feats[...].reshape(feat * n, cols)
        for t in range(w // TILE):
            acc = dot(flat, w_one[:, h * w + t * TILE : h * w + (t + 1) * TILE])
            for f in range(feat):
                part = acc[f * n : (f + 1) * n]
                rows = slice((f // 2) * n, (f // 2 + 1) * n)
                lanes = slice(t * TILE, (t + 1) * TILE)
                proj[h, f % 2, rows, lanes] = part
                projb[h, f % 2, rows, lanes] = part.astype(BF)

    def core_send(h):
        return send(projb.at[h, 1 - c], r1.at[h], mate)

    def y_send(h):
        for j in range(ny):
            rows = slice(j * n, (j + 1) * n)
            qb[h, j] = (proj[h, c, rows] + r1[h, rows].astype(F32)).astype(BF)
        mine = pl.ds(pl.multiple_of(y * n, n), n)
        q[h] = proj[h, c, mine] + r1[h, mine].astype(F32)
        return [
            send(qb.at[h, lax.rem(y + o, ny)], r2.at[h, o - 1], ypeers[o - 1])
            for o in range(1, ny)
        ]

    def owned(h):
        total = q[h]
        for o in range(ny - 1):
            total = total + r2[h, o].astype(F32)
        return total

    def wait(items):
        for item in items:
            item.wait_recv()

    def slot(p):
        return pl.ds(pl.multiple_of(p * SLOT, SLOT), SLOT)

    def table_slot(p):
        return pl.ds(pl.multiple_of(n + p * SLOT, SLOT), SLOT)

    def trade_rows(values, boxes, table):
        table[:n] = values
        boxes[...] = dot(sm[...], values).astype(BF)
        table[table_slot(di)] = boxes[slot(di)]
        return [send(boxes.at[slot(p)], table.at[table_slot(di)], (fi, p)) for p in dpeers]

    def trade_back(values, outgoing, returned):
        terms = dot(ct[...], (values * inv[...]).astype(BF))
        outgoing[...] = terms[n:].astype(BF)
        returned[slot(di)] = outgoing[slot(di)]
        moves = [send(outgoing.at[slot(p)], returned.at[slot(di)], (fi, p)) for p in dpeers]
        return terms[:n], moves

    def pass_on(low, f, k, device):
        block = dp.at[low, f, :, k * TILE : (k + 1) * TILE]
        return send(block, block, device)

    def y_source(o):
        return lax.rem(y - o + ny, ny) * 2 + c

    def gather_start(k):
        to_pair = pass_on(zlow, fi, k, pair)
        to_y = [pass_on(zlow, fi, k, device) for device in ypeers]
        return [to_pair], to_y, [pass_on(zlow, fi, k, mate)]

    def gather_forward(k, to_pair, to_y, to_mate):
        if k % 2:
            to_pair[0].wait_recv()
            far = [pass_on(1 - zlow, fi, k, device) for device in ypeers]
            to_mate.append(pass_on(1 - zlow, fi, k, mate))
            return far, to_y, to_mate
        for o in range(1, ny):
            to_y[o - 1].wait_recv()
            to_pair.append(pass_on(zlow, y_source(o), k, pair))
            to_mate.append(pass_on(zlow, y_source(o), k, mate))
        return to_pair, to_y, to_mate

    def gather_end(k, later, to_y, to_mate):
        if k % 2:
            for low, moves in ((zlow, to_y), (1 - zlow, later)):
                for o in range(1, ny):
                    moves[o - 1].wait_recv()
                    to_mate.append(pass_on(low, y_source(o), k, mate))
            return to_mate
        for o in range(ny):
            later[o].wait_recv()
            to_mate.append(pass_on(1 - zlow, y_source(o), k, mate))
        return to_mate

    for item in first_loads:
        item.wait()
    project(1)
    pl.semaphore_wait(barrier, len(everyone))
    near_core = core_send(1)
    far_cols = pl.ds(pl.multiple_of((1 - zlow) * half_cols, 128), half_cols)
    near_cols = pl.ds(pl.multiple_of(zlow * half_cols, 128), half_cols)
    features_move = send(feats.at[:, :, far_cols], fx, pair)
    self_load.wait()
    project(0)
    self_core = core_send(0)
    near_core.wait_recv()
    near_y = y_send(1)
    self_core.wait_recv()
    self_y = y_send(0)

    for item in later_loads:
        item.wait()
    eye = lax.broadcasted_iota(jnp.int32, (n, n), 0) == lax.broadcasted_iota(jnp.int32, (n, n), 1)
    inv[...] = 1.0 / jnp.sum(jnp.where(eye, deg[...].astype(F32), 0.0), axis=1, keepdims=True)
    entry = lax.broadcasted_iota(jnp.int32, (n + parts * SLOT, n), 0)
    extra = entry - n
    code = jnp.where(
        entry < n, entry,
        jnp.where(extra % SLOT < kmax, n + (extra // SLOT) * kmax + extra % SLOT, -2),
    )
    counts = jnp.zeros(code.shape, F32)
    for s in range(fan):
        used = jnp.where(s < deg[...], nbr[s], -1)
        counts = counts + jnp.where(used == code, 1.0, 0.0)
    ct[...] = counts.astype(BF)
    cm[...] = counts.T.astype(BF)
    edge = (parts * SLOT, parts)
    owner = lax.broadcasted_iota(jnp.int32, edge, 0) // SLOT == lax.broadcasted_iota(jnp.int32, edge, 1)
    spread_rows = dot(jnp.where(owner, 1.0, 0.0).astype(BF), sends[...].astype(F32).astype(BF))
    place = (parts * SLOT, kmax)
    here = lax.broadcasted_iota(jnp.int32, place, 0) % SLOT == lax.broadcasted_iota(jnp.int32, place, 1)
    chosen = jnp.sum(jnp.where(here, spread_rows + 1.0, 0.0), axis=1, keepdims=True) - 1.0
    lane = lax.broadcasted_iota(jnp.int32, (parts * SLOT, n), 1).astype(F32)
    picks = jnp.where(chosen == lane, 1.0, 0.0)
    sm[...] = picks.astype(BF)
    st[...] = picks.T.astype(BF)
    dcat = dot_nt(grads[...], w_two[...])
    dcs[...] = dcat[:, :w]
    local, back_agg = trade_back(dcat[:, w:], k0, h0)
    dcs[...] += local
    ft[zlow] = feats[:, :, near_cols].reshape(feat * n, half_cols).T

    wait(near_y)
    rows_near = trade_rows(owned(1).astype(BF), b1, t1)
    wait(self_y)
    pself[...] = owned(0)
    wait(back_agg)
    dh[...] = dcs[...] + dot(st[...], h0[...])
    wait(rows_near)
    pre = pself[...] + dot(cm[...], t1[...]) * inv[...]
    sig = 1.0 / (1.0 + jnp.exp(-pre))
    d_pre = dh[...] * sig * (1.0 + pre * (1.0 - sig))
    dp[zlow, fi, :, :w] = d_pre.astype(BF)
    chunks = 2 * w // TILE
    half = chunks // 2
    gathers = {}
    near_local, back_pre = trade_back(d_pre, k1, h1)
    dnl[...] = near_local
    for k in range(half):
        gathers[k] = gather_start(k)
    hidden = (pre * sig).astype(BF)
    joined[:, :w] = hidden
    rows_hidden = trade_rows(hidden, b2, t2)

    features_move.wait_recv()
    ft[1 - zlow] = fx[...].reshape(feat * n, half_cols).T
    wait(back_pre)
    dp[zlow, fi, :, w:] = (dnl[...] + dot(st[...], h1[...])).astype(BF)
    for k in range(half, chunks):
        gathers[k] = gather_start(k)
    for k in range(half):
        gathers[k] = gather_forward(k, *gathers[k])

    wait(rows_hidden)
    agg = dot(cm[...], t2[...]) * inv[...]
    joined[:, w:] = agg.astype(BF)
    both = joined[...]
    out[0] = dot(both, w_two[...]).astype(BF)
    span = two.shape[0] // feat
    two_part = dot(both.T, grads[...]).astype(BF)
    for f in range(feat):
        ts[f % 2, (f // 2) * span : (f // 2 + 1) * span] = two_part[f * span : (f + 1) * span]
    two_core = send(ts.at[1 - c], u1, mate)

    for k in range(half, chunks):
        gathers[k] = gather_forward(k, *gathers[k])
    for k in range(half):
        gathers[k] = gather_end(k, *gathers[k])

    rows_x = half_cols // nx
    rows_z = rows_x // (nz // 2)

    def lanes_of(k):
        return slice(k * TILE, (k + 1) * TILE)

    def chunk(k):
        lanes = lanes_of(k)
        g[:, lanes] = (
            dot(ft[0], dp[0, :, :, lanes].reshape(feat * n, TILE))
            + dot(ft[1], dp[1, :, :, lanes].reshape(feat * n, TILE))
        ).astype(BF)
        return [
            send(g.at[pl.ds(pl.multiple_of(t * rows_x, SLOT), rows_x), lanes],
                 rx.at[o, :, lanes], (fi, z * nx + t))
            for o, t in enumerate(xpeers)
        ]

    def z_scatter(k, moves):
        wait(moves)
        lanes = lanes_of(k)
        total = g[pl.ds(pl.multiple_of(x * rows_x, SLOT), rows_x), lanes].astype(F32)
        for o in range(nx - 1):
            total = total + rx[o, :, lanes].astype(F32)
        sx[:, lanes] = total.astype(BF)
        return [
            send(sx.at[pl.ds(pl.multiple_of((t // 2) * rows_z, SLOT), rows_z), lanes],
                 rz.at[o, :, lanes], (fi, t * nx + x))
            for o, t in enumerate(zpeers)
        ]

    def piece(k, low, at):
        return one.at[pl.ds(pl.multiple_of(low * half_cols + at * rows_x, SLOT), rows_x), lanes_of(k)]

    def z_gather(k, moves):
        wait(moves)
        lanes = lanes_of(k)
        total = sx[pl.ds(pl.multiple_of(zhigh * rows_z, SLOT), rows_z), lanes].astype(F32)
        for o in range(nz // 2 - 1):
            total = total + rz[o, :, lanes].astype(F32)
        mine = pl.ds(
            pl.multiple_of(zlow * half_cols + x * rows_x + zhigh * rows_z, SLOT), rows_z
        )
        one[mine, lanes] = total.astype(BF)
        return [send(one.at[mine, lanes], one.at[mine, lanes], (fi, t * nx + x)) for t in zpeers]

    def first_gather(k, moves):
        wait(moves)
        mine = piece(k, zlow, x)
        to_x = [send(mine, mine, (fi, z * nx + t)) for t in xpeers]
        return to_x, send(mine, mine, pair)

    def last_gather(k, moves):
        to_x, to_pair = moves
        rest = []
        if k % 2:
            to_pair.wait_recv()
            got = piece(k, 1 - zlow, x)
            rest = [send(got, got, (fi, z * nx + t)) for t in xpeers]
            return to_x + rest
        for o in range(1, nx):
            to_x[o - 1].wait_recv()
            got = piece(k, zlow, lax.rem(x - o + nx, nx))
            rest.append(send(got, got, pair))
        return [to_pair] + rest

    lanes_x = w // nx
    span_z = span // nz
    allz = [lax.rem(z + o, nz) for o in range(1, nz)]
    my_lanes = pl.ds(pl.multiple_of(x * lanes_x, 128), lanes_x)

    def two_y():
        two_core.wait_recv()
        ub[...] = (ts[c].astype(F32) + u1[...].astype(F32)).astype(BF)
        return [
            send(ub.at[pl.ds(pl.multiple_of(lax.rem(y + o, ny) * span, SLOT), span)],
                 u2.at[o - 1], ypeers[o - 1])
            for o in range(1, ny)
        ]

    def two_x(moves):
        wait(moves)
        total = ub[pl.ds(pl.multiple_of(y * span, SLOT), span)].astype(F32)
        for o in range(ny - 1):
            total = total + u2[o].astype(F32)
        for t in range(nx):
            v[t] = total[:, t * lanes_x : (t + 1) * lanes_x].astype(BF)
        return [send(v.at[t], vx.at[o], (fi, z * nx + t)) for o, t in enumerate(xpeers)]

    def two_z(moves):
        wait(moves)
        total = v[x].astype(F32)
        for o in range(nx - 1):
            total = total + vx[o].astype(F32)
        vs[...] = total.astype(BF)
        return [
            send(vs.at[pl.ds(pl.multiple_of(t * span_z, SLOT), span_z)], vz.at[o], (fi, t * nx + x))
            for o, t in enumerate(allz)
        ]

    def two_zg(moves):
        wait(moves)
        total = vs[pl.ds(pl.multiple_of(z * span_z, SLOT), span_z)].astype(F32)
        for o in range(nz - 1):
            total = total + vz[o].astype(F32)
        mine = pl.ds(pl.multiple_of(fi * span + z * span_z, SLOT), span_z)
        two[mine, my_lanes] = total.astype(BF)
        piece = two.at[mine, my_lanes]
        return [send(piece, piece, (fi, t * nx + x)) for t in allz]

    def two_xg(moves):
        wait(moves)
        piece = two.at[pl.ds(pl.multiple_of(fi * span, SLOT), span), my_lanes]
        return [send(piece, piece, (fi, z * nx + t)) for t in xpeers]

    def two_yg(moves):
        wait(moves)
        piece = two.at[pl.ds(pl.multiple_of(fi * span, SLOT), span)]
        return [send(piece, piece, device) for device in ypeers], send(piece, piece, mate)

    def two_across(moves):
        across = []
        for o in range(1, ny):
            moves[o - 1].wait_recv()
            source = lax.rem(y - o + ny, ny) * 2 + c
            piece = two.at[pl.ds(pl.multiple_of(source * span, SLOT), span)]
            across.append(send(piece, piece, mate))
        return across

    moves = {}
    two_moves = two_y()
    for k in range(half):
        wait(gathers[k])
        moves[k] = chunk(k)
    for k in range(half, chunks):
        gathers[k] = gather_end(k, *gathers[k])
    two_moves = two_x(two_moves)
    for k in range(half, chunks):
        wait(gathers[k])
        moves[k] = chunk(k)
    stages = [z_scatter, z_gather, first_gather, last_gather]
    two_stages = [two_z, two_zg, two_xg]
    for step in range(chunks + len(stages) - 1):
        for s in reversed(range(len(stages))):
            k = step - s
            if 0 <= k < chunks:
                moves[k] = stages[s](k, moves[k])
        if step < len(two_stages):
            two_moves = two_stages[step](two_moves)
        elif step == len(two_stages):
            two_moves, two_mate = two_yg(two_moves)
        elif step == len(two_stages) + 1:
            two_moves = two_across(two_moves)
    for k in range(chunks):
        wait(moves[k])
    wait(two_moves)
    two_mate.wait_recv()
    for copy in copies:
        copy.wait_send()


def finish(scale, out, one, two, out_hbm, one_hbm, two_hbm, one_wide, two_wide, sem):
    copies = [pltpu.make_async_copy(out, out_hbm, sem.at[0])]
    copies[0].start()
    for narrow, wide, target in ((one, one_wide, one_hbm), (two, two_wide, two_hbm)):
        rows = narrow.shape[0] // 4
        for k in range(4):
            part = slice(k * rows, (k + 1) * rows)
            wide[part] = narrow[part].astype(F32) * scale
            copy = pltpu.make_async_copy(wide.at[part], target.at[part], sem.at[len(copies)])
            copy.start()
            copies.append(copy)
    for copy in copies:
        copy.wait()


def on_device(nx, nz, features, w_one, w_two, neighbor, degree, send_rows, grad_out):
    feat, n, cols = features.shape
    w = w_two.shape[1]
    ny = feat // 2
    parts, kmax = send_rows.shape[1:]
    table = n + parts * SLOT
    edge = parts * SLOT
    half_cols = cols // 2
    rows_x = half_cols // nx
    rows_z = rows_x // (nz // 2)
    span = 2 * w // feat
    lanes_x = w // nx
    chunks = 2 * w // TILE
    n_copies = (
        3 + 2 * (ny - 1) + 4 * (parts - 1)
        + chunks * (4 * ny + 2 + 4 * nx + nz)
        + 2 + 4 * ny + 2 * (nx + nz)
    )
    vm = pltpu.VMEM
    scratch = [
        vm(features.shape, BF), vm(w_one.shape, BF), vm(w_two.shape, BF),
        vm((neighbor.shape[2], 1, n), jnp.int32), vm((1, n), jnp.int32),
        vm((parts, kmax), jnp.int32), vm((n, w), BF),
        vm((2, 2, ny * n, w), F32), vm((2, 2, ny * n, w), BF), vm((2, ny * n, w), BF),
        vm((2, n, w), F32), vm((2, ny, n, w), BF), vm((2, ny - 1, n, w), BF),
        vm((n, table), BF), vm((table, n), BF), vm((edge, n), BF), vm((n, edge), BF),
        vm((table, w), BF), vm((table, w), BF), vm((edge, w), BF), vm((edge, w), BF),
        vm((edge, w), BF), vm((edge, w), BF), vm((edge, w), BF), vm((edge, w), BF),
        vm((n, 1), F32), vm((n, w), F32), vm((n, w), F32), vm((n, w), F32), vm((n, w), F32),
        vm((n, 2 * w), BF), vm((feat, n, half_cols), BF), vm((2, half_cols, feat * n), BF),
        vm((2, feat, n, 2 * w), BF),
        vm((half_cols, 2 * w), BF), vm((nx - 1, rows_x, 2 * w), BF), vm((rows_x, 2 * w), BF),
        vm((nz // 2 - 1, rows_z, 2 * w), BF),
        vm((2, ny * span, w), BF), vm((ny * span, w), BF), vm((ny * span, w), BF),
        vm((ny - 1, span, w), BF), vm((nx, span, lanes_x), BF), vm((nx - 1, span, lanes_x), BF),
        vm((span, lanes_x), BF), vm((nz - 1, span // nz, lanes_x), BF),
        pltpu.SemaphoreType.DMA((n_copies,)), pltpu.SemaphoreType.DMA((n_copies,)),
        pltpu.SemaphoreType.DMA((8,)),
    ]
    spec = pl.BlockSpec(memory_space=pltpu.VMEM)
    hbm = pl.BlockSpec(memory_space=pltpu.HBM)
    out, one_sum, two_sum = pl.pallas_call(
        functools.partial(kernel, feat, nx, nz, kmax),
        out_shape=(
            jax.ShapeDtypeStruct((1, n, w), BF),
            jax.ShapeDtypeStruct((cols, 2 * w), BF),
            jax.ShapeDtypeStruct((2 * w, w), BF),
        ),
        in_specs=[hbm] * 7,
        out_specs=(spec, spec, spec),
        scratch_shapes=scratch,
        compiler_params=pltpu.CompilerParams(
            collective_id=0, has_side_effects=True, vmem_limit_bytes=40 * 1024 * 1024
        ),
    )(*(
        pltpu.with_memory_space_constraint(operand, pltpu.HBM)
        for operand in (
            features, w_one, w_two, jnp.transpose(neighbor, (2, 0, 1)), degree, send_rows[0],
            grad_out[0],
        )
    ))
    scale = 1.0 / math.sqrt(feat * n * parts)
    wide = (
        jax.ShapeDtypeStruct(out.shape, BF),
        jax.ShapeDtypeStruct(one_sum.shape, F32),
        jax.ShapeDtypeStruct(two_sum.shape, F32),
    )
    return pl.pallas_call(
        functools.partial(finish, scale),
        out_shape=wide,
        in_specs=[spec] * 3,
        out_specs=(hbm, hbm, hbm),
        scratch_shapes=[
            vm(one_sum.shape, F32), vm(two_sum.shape, F32), pltpu.SemaphoreType.DMA((9,)),
        ],
        compiler_params=pltpu.CompilerParams(vmem_limit_bytes=16 * 1024 * 1024),
    )(out, one_sum, two_sum)


def solution(mesh):
    parts = mesh.shape["dom"]
    nx = 1 << ((parts.bit_length() - 2) // 2)
    in_specs = (
        P(None, "dom", "feat"),
        P("feat", None),
        P(),
        P("feat", "dom", None),
        P("feat", "dom"),
        P("feat", "dom", None),
        P("feat", "dom", None),
    )
    out_specs = (P("feat", "dom", None), P("feat", None), P())
    return jax.shard_map(
        functools.partial(on_device, nx, parts // nx),
        mesh=mesh, in_specs=in_specs, out_specs=out_specs, check_vma=False,
    )
```

```python
import functools
import math

import jax
import jax.numpy as jnp
from jax import lax
from jax.experimental import pallas as pl
from jax.experimental.pallas import tpu as pltpu
from jax.sharding import PartitionSpec as P

BF = jnp.bfloat16
F32 = jnp.float32
SLOT = 16
TILE = 256


def dot(a, b):
    return jnp.dot(a, b, preferred_element_type=F32)


def dot_nt(a, b):
    return lax.dot_general(a, b, (((1,), (1,)), ((), ())), preferred_element_type=F32)


def kernel(
    feat, nx, nz, kmax,
    feats_hbm, w_one_hbm, w_two_hbm, nbr_hbm, deg_hbm, sends_hbm, grads_hbm,
    out, one, two,
    feats, w_one, w_two, nbr, deg, sends, grads,
    proj, projb, r1, q, qb, r2, cm, ct, sm, st, t1, t2, b1, b2, k0, k1, h0, h1,
    inv, dcs, dh, pself, dnl, joined, fx, ft, dp, g, rx, rz, ts, u1, ub, u2, v, vx, vs, vz,
    ssem, rsem, lsem,
):
    ny = feat // 2
    parts = nx * nz
    n = nbr.shape[2]
    w = grads.shape[1]
    cols = w_one.shape[0]
    fan = nbr.shape[0]
    half_cols = cols // 2
    fi = lax.axis_index("feat")
    di = lax.axis_index("dom")
    y, c = fi // 2, fi % 2
    z, x = di // nx, di % nx
    mate = (y * 2 + 1 - c, di)
    zlow, zhigh = z % 2, z // 2
    pair = (fi, (z + 1 - 2 * zlow) * nx + x)
    count = [0]

    def send(src, dst, device):
        k = count[0]
        count[0] += 1
        copy = pltpu.make_async_remote_copy(
            src_ref=src, dst_ref=dst, send_sem=ssem.at[k], recv_sem=rsem.at[k],
            device_id=device, device_id_type=pl.DeviceIdType.MESH,
        )
        copy.start()
        copies.append(copy)
        return copy

    copies = []
    ypeers = [(lax.rem(y + o, ny) * 2 + c, di) for o in range(1, ny)]
    dpeers = [lax.rem(di + o, parts) for o in range(1, parts)]
    xpeers = [lax.rem(x + o, nx) for o in range(1, nx)]
    zpeers = [lax.rem(zhigh + o, nz // 2) * 2 + zlow for o in range(1, nz // 2)]

    barrier = pltpu.get_barrier_semaphore()
    everyone = [mate] + ypeers + [(fi, p) for p in dpeers]
    for device in everyone:
        pl.semaphore_signal(barrier, inc=1, device_id=device, device_id_type=pl.DeviceIdType.MESH)

    def load(k, src, dst):
        copy = pltpu.make_async_copy(src, dst, lsem.at[k])
        copy.start()
        return copy

    first_loads = [load(0, w_one_hbm.at[:, w:], w_one.at[:, w:]), load(1, feats_hbm, feats)]
    self_load = load(2, w_one_hbm.at[:, :w], w_one.at[:, :w])
    later_loads = [
        load(3, nbr_hbm, nbr), load(4, deg_hbm, deg), load(5, sends_hbm, sends),
        load(6, grads_hbm, grads), load(7, w_two_hbm, w_two),
    ]

    def project(h):
        flat = feats[...].reshape(feat * n, cols)
        for t in range(w // TILE):
            acc = dot(flat, w_one[:, h * w + t * TILE : h * w + (t + 1) * TILE])
            for f in range(feat):
                part = acc[f * n : (f + 1) * n]
                rows = slice((f // 2) * n, (f // 2 + 1) * n)
                lanes = slice(t * TILE, (t + 1) * TILE)
                proj[h, f % 2, rows, lanes] = part
                projb[h, f % 2, rows, lanes] = part.astype(BF)

    def core_send(h):
        return send(projb.at[h, 1 - c], r1.at[h], mate)

    def y_send(h):
        for j in range(ny):
            rows = slice(j * n, (j + 1) * n)
            qb[h, j] = (proj[h, c, rows] + r1[h, rows].astype(F32)).astype(BF)
        mine = pl.ds(pl.multiple_of(y * n, n), n)
        q[h] = proj[h, c, mine] + r1[h, mine].astype(F32)
        return [
            send(qb.at[h, lax.rem(y + o, ny)], r2.at[h, o - 1], ypeers[o - 1])
            for o in range(1, ny)
        ]

    def owned(h):
        total = q[h]
        for o in range(ny - 1):
            total = total + r2[h, o].astype(F32)
        return total

    def wait(items):
        for item in items:
            item.wait_recv()

    def slot(p):
        return pl.ds(pl.multiple_of(p * SLOT, SLOT), SLOT)

    def table_slot(p):
        return pl.ds(pl.multiple_of(n + p * SLOT, SLOT), SLOT)

    def trade_rows(values, boxes, table):
        table[:n] = values
        boxes[...] = dot(sm[...], values).astype(BF)
        table[table_slot(di)] = boxes[slot(di)]
        return [send(boxes.at[slot(p)], table.at[table_slot(di)], (fi, p)) for p in dpeers]

    def trade_back(values, outgoing, returned):
        terms = dot(ct[...], (values * inv[...]).astype(BF))
        outgoing[...] = terms[n:].astype(BF)
        returned[slot(di)] = outgoing[slot(di)]
        moves = [send(outgoing.at[slot(p)], returned.at[slot(di)], (fi, p)) for p in dpeers]
        return terms[:n], moves

    def pass_on(low, f, k, device):
        block = dp.at[low, f, :, k * TILE : (k + 1) * TILE]
        return send(block, block, device)

    def y_source(o):
        return lax.rem(y - o + ny, ny) * 2 + c

    def gather_start(k):
        to_pair = pass_on(zlow, fi, k, pair)
        to_y = [pass_on(zlow, fi, k, device) for device in ypeers]
        return [to_pair], to_y, [pass_on(zlow, fi, k, mate)]

    def gather_forward(k, to_pair, to_y, to_mate):
        if k % 2:
            to_pair[0].wait_recv()
            far = [pass_on(1 - zlow, fi, k, device) for device in ypeers]
            to_mate.append(pass_on(1 - zlow, fi, k, mate))
            return far, to_y, to_mate
        for o in range(1, ny):
            to_y[o - 1].wait_recv()
            to_pair.append(pass_on(zlow, y_source(o), k, pair))
            to_mate.append(pass_on(zlow, y_source(o), k, mate))
        return to_pair, to_y, to_mate

    def gather_end(k, later, to_y, to_mate):
        if k % 2:
            for low, moves in ((zlow, to_y), (1 - zlow, later)):
                for o in range(1, ny):
                    moves[o - 1].wait_recv()
                    to_mate.append(pass_on(low, y_source(o), k, mate))
            return to_mate
        for o in range(ny):
            later[o].wait_recv()
            to_mate.append(pass_on(1 - zlow, y_source(o), k, mate))
        return to_mate

    first_loads[1].wait()
    pl.semaphore_wait(barrier, len(everyone))
    far_cols = pl.ds(pl.multiple_of((1 - zlow) * half_cols, 128), half_cols)
    near_cols = pl.ds(pl.multiple_of(zlow * half_cols, 128), half_cols)
    features_move = send(feats.at[:, :, far_cols], fx, pair)
    first_loads[0].wait()
    project(1)
    near_core = core_send(1)
    self_load.wait()
    project(0)
    self_core = core_send(0)
    near_core.wait_recv()
    near_y = y_send(1)
    self_core.wait_recv()
    self_y = y_send(0)

    for item in later_loads:
        item.wait()
    eye = lax.broadcasted_iota(jnp.int32, (n, n), 0) == lax.broadcasted_iota(jnp.int32, (n, n), 1)
    inv[...] = 1.0 / jnp.sum(jnp.where(eye, deg[...].astype(F32), 0.0), axis=1, keepdims=True)
    entry = lax.broadcasted_iota(jnp.int32, (n + parts * SLOT, n), 0)
    extra = entry - n
    code = jnp.where(
        entry < n, entry,
        jnp.where(extra % SLOT < kmax, n + (extra // SLOT) * kmax + extra % SLOT, -2),
    )
    counts = jnp.zeros(code.shape, F32)
    for s in range(fan):
        used = jnp.where(s < deg[...], nbr[s], -1)
        counts = counts + jnp.where(used == code, 1.0, 0.0)
    ct[...] = counts.astype(BF)
    cm[...] = counts.T.astype(BF)
    edge = (parts * SLOT, parts)
    owner = lax.broadcasted_iota(jnp.int32, edge, 0) // SLOT == lax.broadcasted_iota(jnp.int32, edge, 1)
    spread_rows = dot(jnp.where(owner, 1.0, 0.0).astype(BF), sends[...].astype(F32).astype(BF))
    place = (parts * SLOT, kmax)
    here = lax.broadcasted_iota(jnp.int32, place, 0) % SLOT == lax.broadcasted_iota(jnp.int32, place, 1)
    chosen = jnp.sum(jnp.where(here, spread_rows + 1.0, 0.0), axis=1, keepdims=True) - 1.0
    lane = lax.broadcasted_iota(jnp.int32, (parts * SLOT, n), 1).astype(F32)
    picks = jnp.where(chosen == lane, 1.0, 0.0)
    sm[...] = picks.astype(BF)
    st[...] = picks.T.astype(BF)
    dcat = dot_nt(grads[...], w_two[...])
    dcs[...] = dcat[:, :w]
    local, back_agg = trade_back(dcat[:, w:], k0, h0)
    dcs[...] += local

    wait(near_y)
    rows_near = trade_rows(owned(1).astype(BF), b1, t1)
    ft[zlow] = feats[:, :, near_cols].reshape(feat * n, half_cols).T
    wait(self_y)
    pself[...] = owned(0)
    wait(back_agg)
    dh[...] = dcs[...] + dot(st[...], h0[...])
    wait(rows_near)
    pre = pself[...] + dot(cm[...], t1[...]) * inv[...]
    sig = 1.0 / (1.0 + jnp.exp(-pre))
    d_pre = dh[...] * sig * (1.0 + pre * (1.0 - sig))
    dp[zlow, fi, :, :w] = d_pre.astype(BF)
    chunks = 2 * w // TILE
    half = chunks // 2
    gathers = {}
    near_local, back_pre = trade_back(d_pre, k1, h1)
    dnl[...] = near_local
    for k in range(half):
        gathers[k] = gather_start(k)
    hidden = (pre * sig).astype(BF)
    joined[:, :w] = hidden
    rows_hidden = trade_rows(hidden, b2, t2)

    features_move.wait_recv()
    ft[1 - zlow] = fx[...].reshape(feat * n, half_cols).T
    wait(back_pre)
    dp[zlow, fi, :, w:] = (dnl[...] + dot(st[...], h1[...])).astype(BF)
    for k in range(half, chunks):
        gathers[k] = gather_start(k)
    for k in range(half):
        gathers[k] = gather_forward(k, *gathers[k])

    wait(rows_hidden)
    agg = dot(cm[...], t2[...]) * inv[...]
    joined[:, w:] = agg.astype(BF)
    both = joined[...]
    out[0] = dot(both, w_two[...]).astype(BF)
    span = two.shape[0] // feat
    two_part = dot(both.T, grads[...]).astype(BF)
    for f in range(feat):
        ts[f % 2, (f // 2) * span : (f // 2 + 1) * span] = two_part[f * span : (f + 1) * span]
    two_core = send(ts.at[1 - c], u1, mate)

    for k in range(half, chunks):
        gathers[k] = gather_forward(k, *gathers[k])
    for k in range(half):
        gathers[k] = gather_end(k, *gathers[k])

    rows_x = half_cols // nx

    def lanes_of(k):
        return slice(k * TILE, (k + 1) * TILE)

    def chunk(k):
        lanes = lanes_of(k)
        g[:, lanes] = (
            dot(ft[0], dp[0, :, :, lanes].reshape(feat * n, TILE))
            + dot(ft[1], dp[1, :, :, lanes].reshape(feat * n, TILE))
        ).astype(BF)
        return [
            send(g.at[pl.ds(pl.multiple_of(t * rows_x, SLOT), rows_x), lanes],
                 rx.at[o, :, lanes], (fi, z * nx + t))
            for o, t in enumerate(xpeers)
        ]

    def z_exchange(k, moves):
        wait(moves)
        lanes = lanes_of(k)
        total = g[pl.ds(pl.multiple_of(x * rows_x, SLOT), rows_x), lanes].astype(F32)
        for o in range(nx - 1):
            total = total + rx[o, :, lanes].astype(F32)
        rz[zhigh, :, lanes] = total.astype(BF)
        part = rz.at[zhigh, :, lanes]
        return [send(part, part, (fi, t * nx + x)) for t in zpeers]

    def piece(k, low, at):
        return one.at[pl.ds(pl.multiple_of(low * half_cols + at * rows_x, SLOT), rows_x), lanes_of(k)]

    def first_gather(k, moves):
        wait(moves)
        lanes = lanes_of(k)
        total = rz[0, :, lanes].astype(F32)
        for o in range(1, nz // 2):
            total = total + rz[o, :, lanes].astype(F32)
        rows = pl.ds(pl.multiple_of(zlow * half_cols + x * rows_x, SLOT), rows_x)
        one[rows, lanes] = total.astype(BF)
        mine = piece(k, zlow, x)
        to_x = [send(mine, mine, (fi, z * nx + t)) for t in xpeers]
        return to_x, send(mine, mine, pair)

    def last_gather(k, moves):
        to_x, to_pair = moves
        rest = []
        if k % 2:
            to_pair.wait_recv()
            got = piece(k, 1 - zlow, x)
            rest = [send(got, got, (fi, z * nx + t)) for t in xpeers]
            return to_x + rest
        for o in range(1, nx):
            to_x[o - 1].wait_recv()
            got = piece(k, zlow, lax.rem(x - o + nx, nx))
            rest.append(send(got, got, pair))
        return [to_pair] + rest

    lanes_x = w // nx
    span_z = span // nz
    allz = [lax.rem(z + o, nz) for o in range(1, nz)]
    my_lanes = pl.ds(pl.multiple_of(x * lanes_x, 128), lanes_x)

    def two_y():
        two_core.wait_recv()
        ub[...] = (ts[c].astype(F32) + u1[...].astype(F32)).astype(BF)
        return [
            send(ub.at[pl.ds(pl.multiple_of(lax.rem(y + o, ny) * span, SLOT), span)],
                 u2.at[o - 1], ypeers[o - 1])
            for o in range(1, ny)
        ]

    def two_x(moves):
        wait(moves)
        total = ub[pl.ds(pl.multiple_of(y * span, SLOT), span)].astype(F32)
        for o in range(ny - 1):
            total = total + u2[o].astype(F32)
        for t in range(nx):
            v[t] = total[:, t * lanes_x : (t + 1) * lanes_x].astype(BF)
        return [send(v.at[t], vx.at[o], (fi, z * nx + t)) for o, t in enumerate(xpeers)]

    def two_z(moves):
        wait(moves)
        total = v[x].astype(F32)
        for o in range(nx - 1):
            total = total + vx[o].astype(F32)
        vs[...] = total.astype(BF)
        return [
            send(vs.at[pl.ds(pl.multiple_of(t * span_z, SLOT), span_z)], vz.at[o], (fi, t * nx + x))
            for o, t in enumerate(allz)
        ]

    def two_zg(moves):
        wait(moves)
        total = vs[pl.ds(pl.multiple_of(z * span_z, SLOT), span_z)].astype(F32)
        for o in range(nz - 1):
            total = total + vz[o].astype(F32)
        mine = pl.ds(pl.multiple_of(fi * span + z * span_z, SLOT), span_z)
        two[mine, my_lanes] = total.astype(BF)
        piece = two.at[mine, my_lanes]
        return [send(piece, piece, (fi, t * nx + x)) for t in allz]

    def two_xg(moves):
        wait(moves)
        piece = two.at[pl.ds(pl.multiple_of(fi * span, SLOT), span), my_lanes]
        return [send(piece, piece, (fi, z * nx + t)) for t in xpeers]

    def two_yg(moves):
        wait(moves)
        piece = two.at[pl.ds(pl.multiple_of(fi * span, SLOT), span)]
        return [send(piece, piece, device) for device in ypeers], send(piece, piece, mate)

    def two_across(moves):
        across = []
        for o in range(1, ny):
            moves[o - 1].wait_recv()
            source = lax.rem(y - o + ny, ny) * 2 + c
            piece = two.at[pl.ds(pl.multiple_of(source * span, SLOT), span)]
            across.append(send(piece, piece, mate))
        return across

    moves = {}
    marks = [len(copies)]
    two_moves = two_y()
    for k in range(half):
        wait(gathers[k])
        moves[k] = chunk(k)
    for k in range(half, chunks):
        gathers[k] = gather_end(k, *gathers[k])
    two_moves = two_x(two_moves)
    for k in range(half, chunks):
        wait(gathers[k])
        moves[k] = chunk(k)
    stages = [z_exchange, first_gather, last_gather]
    drained = 0
    two_stages = [two_z, two_zg, two_xg]
    for step in range(chunks + len(stages) - 1):
        marks.append(len(copies))
        for s in reversed(range(len(stages))):
            k = step - s
            if 0 <= k < chunks:
                moves[k] = stages[s](k, moves[k])
        if step < len(two_stages):
            two_moves = two_stages[step](two_moves)
        elif step == len(two_stages):
            two_moves, two_mate = two_yg(two_moves)
        elif step == len(two_stages) + 1:
            two_moves = two_across(two_moves)
        settled = marks[max(step - 1, 0)]
        for copy in copies[drained:settled]:
            copy.wait_send()
        drained = settled
    for k in range(chunks):
        wait(moves[k])
    wait(two_moves)
    two_mate.wait_recv()
    for copy in copies[drained:]:
        copy.wait_send()


def finish(scale, out, one, two, out_hbm, one_hbm, two_hbm, one_wide, two_wide, sem):
    copies = [pltpu.make_async_copy(out, out_hbm, sem.at[0])]
    copies[0].start()
    for narrow, wide, target in ((one, one_wide, one_hbm), (two, two_wide, two_hbm)):
        rows = narrow.shape[0] // 4
        for k in range(4):
            part = slice(k * rows, (k + 1) * rows)
            wide[part] = narrow[part].astype(F32) * scale
            copy = pltpu.make_async_copy(wide.at[part], target.at[part], sem.at[len(copies)])
            copy.start()
            copies.append(copy)
    for copy in copies:
        copy.wait()


def on_device(nx, nz, features, w_one, w_two, neighbor, degree, send_rows, grad_out):
    feat, n, cols = features.shape
    w = w_two.shape[1]
    ny = feat // 2
    parts, kmax = send_rows.shape[1:]
    table = n + parts * SLOT
    edge = parts * SLOT
    half_cols = cols // 2
    rows_x = half_cols // nx
    span = 2 * w // feat
    lanes_x = w // nx
    chunks = 2 * w // TILE
    n_copies = (
        3 + 2 * (ny - 1) + 4 * (parts - 1)
        + chunks * (4 * ny + 2 + 4 * nx + nz)
        + 2 + 4 * ny + 2 * (nx + nz)
    )
    vm = pltpu.VMEM
    scratch = [
        vm(features.shape, BF), vm(w_one.shape, BF), vm(w_two.shape, BF),
        vm((neighbor.shape[2], 1, n), jnp.int32), vm((1, n), jnp.int32),
        vm((parts, kmax), jnp.int32), vm((n, w), BF),
        vm((2, 2, ny * n, w), F32), vm((2, 2, ny * n, w), BF), vm((2, ny * n, w), BF),
        vm((2, n, w), F32), vm((2, ny, n, w), BF), vm((2, ny - 1, n, w), BF),
        vm((n, table), BF), vm((table, n), BF), vm((edge, n), BF), vm((n, edge), BF),
        vm((table, w), BF), vm((table, w), BF), vm((edge, w), BF), vm((edge, w), BF),
        vm((edge, w), BF), vm((edge, w), BF), vm((edge, w), BF), vm((edge, w), BF),
        vm((n, 1), F32), vm((n, w), F32), vm((n, w), F32), vm((n, w), F32), vm((n, w), F32),
        vm((n, 2 * w), BF), vm((feat, n, half_cols), BF), vm((2, half_cols, feat * n), BF),
        vm((2, feat, n, 2 * w), BF),
        vm((half_cols, 2 * w), BF), vm((nx - 1, rows_x, 2 * w), BF),
        vm((nz // 2, rows_x, 2 * w), BF),
        vm((2, ny * span, w), BF), vm((ny * span, w), BF), vm((ny * span, w), BF),
        vm((ny - 1, span, w), BF), vm((nx, span, lanes_x), BF), vm((nx - 1, span, lanes_x), BF),
        vm((span, lanes_x), BF), vm((nz - 1, span // nz, lanes_x), BF),
        pltpu.SemaphoreType.DMA((n_copies,)), pltpu.SemaphoreType.DMA((n_copies,)),
        pltpu.SemaphoreType.DMA((8,)),
    ]
    spec = pl.BlockSpec(memory_space=pltpu.VMEM)
    hbm = pl.BlockSpec(memory_space=pltpu.HBM)
    out, one_sum, two_sum = pl.pallas_call(
        functools.partial(kernel, feat, nx, nz, kmax),
        out_shape=(
            jax.ShapeDtypeStruct((1, n, w), BF),
            jax.ShapeDtypeStruct((cols, 2 * w), BF),
            jax.ShapeDtypeStruct((2 * w, w), BF),
        ),
        in_specs=[hbm] * 7,
        out_specs=(spec, spec, spec),
        scratch_shapes=scratch,
        compiler_params=pltpu.CompilerParams(
            collective_id=0, has_side_effects=True, vmem_limit_bytes=40 * 1024 * 1024
        ),
    )(*(
        pltpu.with_memory_space_constraint(operand, pltpu.HBM)
        for operand in (
            features, w_one, w_two, jnp.transpose(neighbor, (2, 0, 1)), degree, send_rows[0],
            grad_out[0],
        )
    ))
    scale = 1.0 / math.sqrt(feat * n * parts)
    wide = (
        jax.ShapeDtypeStruct(out.shape, BF),
        jax.ShapeDtypeStruct(one_sum.shape, F32),
        jax.ShapeDtypeStruct(two_sum.shape, F32),
    )
    return pl.pallas_call(
        functools.partial(finish, scale),
        out_shape=wide,
        in_specs=[spec] * 3,
        out_specs=(hbm, hbm, hbm),
        scratch_shapes=[
            vm(one_sum.shape, F32), vm(two_sum.shape, F32), pltpu.SemaphoreType.DMA((9,)),
        ],
        compiler_params=pltpu.CompilerParams(vmem_limit_bytes=16 * 1024 * 1024),
    )(out, one_sum, two_sum)


def solution(mesh):
    parts = mesh.shape["dom"]
    nx = 1 << ((parts.bit_length() - 2) // 2)
    in_specs = (
        P(None, "dom", "feat"),
        P("feat", None),
        P(),
        P("feat", "dom", None),
        P("feat", "dom"),
        P("feat", "dom", None),
        P("feat", "dom", None),
    )
    out_specs = (P("feat", "dom", None), P("feat", None), P())
    return jax.shard_map(
        functools.partial(on_device, nx, parts // nx),
        mesh=mesh, in_specs=in_specs, out_specs=out_specs, check_vma=False,
    )
```

```python
import functools
import math

import jax
import jax.numpy as jnp
from jax import lax
from jax.experimental import pallas as pl
from jax.experimental.pallas import tpu as pltpu
from jax.sharding import PartitionSpec as P

BF = jnp.bfloat16
F32 = jnp.float32
SLOT = 16
TILE = 256


def dot(a, b):
    return jnp.dot(a, b, preferred_element_type=F32)


def dot_nt(a, b):
    return lax.dot_general(a, b, (((1,), (1,)), ((), ())), preferred_element_type=F32)


def kernel(
    feat, nx, nz, kmax,
    feats_hbm, w_one_hbm, w_two_hbm, nbr_hbm, deg_hbm, sends_hbm, grads_hbm,
    out, one, two,
    feats, w_one, w_two, nbr, deg, sends, grads,
    proj, projb, r1, q, qb, r2, cm, ct, sm, st, t1, t2, b1, b2, k0, k1, h0, h1,
    inv, dcs, dh, pself, dnl, joined, fx, ft, dp, g, rx, rz, ts, u1, ub, u2, v, vx, vs, vz,
    ssem, rsem, lsem,
):
    ny = feat // 2
    parts = nx * nz
    n = nbr.shape[2]
    w = grads.shape[1]
    cols = w_one.shape[0]
    fan = nbr.shape[0]
    half_cols = cols // 2
    fi = lax.axis_index("feat")
    di = lax.axis_index("dom")
    y, c = fi // 2, fi % 2
    z, x = di // nx, di % nx
    mate = (y * 2 + 1 - c, di)
    zlow, zhigh = z % 2, z // 2
    pair = (fi, (z + 1 - 2 * zlow) * nx + x)
    count = [0]

    def send(src, dst, device):
        k = count[0]
        count[0] += 1
        copy = pltpu.make_async_remote_copy(
            src_ref=src, dst_ref=dst, send_sem=ssem.at[k], recv_sem=rsem.at[k],
            device_id=device, device_id_type=pl.DeviceIdType.MESH,
        )
        copy.start()
        copies.append(copy)
        return copy

    copies = []
    ypeers = [(lax.rem(y + o, ny) * 2 + c, di) for o in range(1, ny)]
    dpeers = [lax.rem(di + o, parts) for o in range(1, parts)]
    xpeers = [lax.rem(x + o, nx) for o in range(1, nx)]
    zpeers = [lax.rem(zhigh + o, nz // 2) * 2 + zlow for o in range(1, nz // 2)]

    barrier = pltpu.get_barrier_semaphore()
    everyone = [mate] + ypeers + [(fi, p) for p in dpeers]
    for device in everyone:
        pl.semaphore_signal(barrier, inc=1, device_id=device, device_id_type=pl.DeviceIdType.MESH)

    def load(k, src, dst):
        copy = pltpu.make_async_copy(src, dst, lsem.at[k])
        copy.start()
        return copy

    first_loads = [load(0, w_one_hbm.at[:, w:], w_one.at[:, w:]), load(1, feats_hbm, feats)]
    self_load = load(2, w_one_hbm.at[:, :w], w_one.at[:, :w])
    later_loads = [
        load(3, nbr_hbm, nbr), load(4, deg_hbm, deg), load(5, sends_hbm, sends),
        load(6, grads_hbm, grads), load(7, w_two_hbm, w_two),
    ]

    def project(h):
        flat = feats[...].reshape(feat * n, cols)
        for t in range(w // TILE):
            acc = dot(flat, w_one[:, h * w + t * TILE : h * w + (t + 1) * TILE])
            for f in range(feat):
                part = acc[f * n : (f + 1) * n]
                rows = slice((f // 2) * n, (f // 2 + 1) * n)
                lanes = slice(t * TILE, (t + 1) * TILE)
                proj[h, f % 2, rows, lanes] = part
                projb[h, f % 2, rows, lanes] = part.astype(BF)

    def core_send(h):
        return send(projb.at[h, 1 - c], r1.at[h], mate)

    def y_send(h):
        for j in range(ny):
            rows = slice(j * n, (j + 1) * n)
            qb[h, j] = (proj[h, c, rows] + r1[h, rows].astype(F32)).astype(BF)
        mine = pl.ds(pl.multiple_of(y * n, n), n)
        q[h] = proj[h, c, mine] + r1[h, mine].astype(F32)
        return [
            send(qb.at[h, lax.rem(y + o, ny)], r2.at[h, o - 1], ypeers[o - 1])
            for o in range(1, ny)
        ]

    def owned(h):
        total = q[h]
        for o in range(ny - 1):
            total = total + r2[h, o].astype(F32)
        return total

    def wait(items):
        for item in items:
            item.wait_recv()

    def slot(p):
        return pl.ds(pl.multiple_of(p * SLOT, SLOT), SLOT)

    def table_slot(p):
        return pl.ds(pl.multiple_of(n + p * SLOT, SLOT), SLOT)

    def trade_rows(values, boxes, table):
        table[:n] = values
        boxes[...] = dot(sm[...], values).astype(BF)
        table[table_slot(di)] = boxes[slot(di)]
        return [send(boxes.at[slot(p)], table.at[table_slot(di)], (fi, p)) for p in dpeers]

    def trade_back(values, outgoing, returned):
        terms = dot(ct[...], (values * inv[...]).astype(BF))
        outgoing[...] = terms[n:].astype(BF)
        returned[slot(di)] = outgoing[slot(di)]
        moves = [send(outgoing.at[slot(p)], returned.at[slot(di)], (fi, p)) for p in dpeers]
        return terms[:n], moves

    def pass_on(low, f, k, device):
        block = dp.at[low, f, k]
        return send(block, block, device)

    def y_source(o):
        return lax.rem(y - o + ny, ny) * 2 + c

    def gather_start(k):
        to_pair = pass_on(zlow, fi, k, pair)
        to_y = [pass_on(zlow, fi, k, device) for device in ypeers]
        return [to_pair], to_y, [pass_on(zlow, fi, k, mate)]

    def gather_forward(k, to_pair, to_y, to_mate):
        if k % 2:
            to_pair[0].wait_recv()
            far = [pass_on(1 - zlow, fi, k, device) for device in ypeers]
            to_mate.append(pass_on(1 - zlow, fi, k, mate))
            return far, to_y, to_mate
        for o in range(1, ny):
            to_y[o - 1].wait_recv()
            to_pair.append(pass_on(zlow, y_source(o), k, pair))
            to_mate.append(pass_on(zlow, y_source(o), k, mate))
        return to_pair, to_y, to_mate

    def gather_end(k, later, to_y, to_mate):
        if k % 2:
            for low, moves in ((zlow, to_y), (1 - zlow, later)):
                for o in range(1, ny):
                    moves[o - 1].wait_recv()
                    to_mate.append(pass_on(low, y_source(o), k, mate))
            return to_mate
        for o in range(ny):
            later[o].wait_recv()
            to_mate.append(pass_on(1 - zlow, y_source(o), k, mate))
        return to_mate

    first_loads[1].wait()
    pl.semaphore_wait(barrier, len(everyone))
    far_cols = pl.ds(pl.multiple_of((1 - zlow) * half_cols, 128), half_cols)
    near_cols = pl.ds(pl.multiple_of(zlow * half_cols, 128), half_cols)
    features_move = send(feats.at[:, :, far_cols], fx, pair)
    first_loads[0].wait()
    project(1)
    near_core = core_send(1)
    self_load.wait()
    project(0)
    self_core = core_send(0)
    near_core.wait_recv()
    near_y = y_send(1)
    self_core.wait_recv()
    self_y = y_send(0)

    for item in later_loads:
        item.wait()
    eye = lax.broadcasted_iota(jnp.int32, (n, n), 0) == lax.broadcasted_iota(jnp.int32, (n, n), 1)
    inv[...] = 1.0 / jnp.sum(jnp.where(eye, deg[...].astype(F32), 0.0), axis=1, keepdims=True)
    entry = lax.broadcasted_iota(jnp.int32, (n + parts * SLOT, n), 0)
    extra = entry - n
    code = jnp.where(
        entry < n, entry,
        jnp.where(extra % SLOT < kmax, n + (extra // SLOT) * kmax + extra % SLOT, -2),
    )
    counts = jnp.zeros(code.shape, F32)
    for s in range(fan):
        used = jnp.where(s < deg[...], nbr[s], -1)
        counts = counts + jnp.where(used == code, 1.0, 0.0)
    ct[...] = counts.astype(BF)
    cm[...] = counts.T.astype(BF)
    edge = (parts * SLOT, parts)
    owner = lax.broadcasted_iota(jnp.int32, edge, 0) // SLOT == lax.broadcasted_iota(jnp.int32, edge, 1)
    spread_rows = dot(jnp.where(owner, 1.0, 0.0).astype(BF), sends[...].astype(F32).astype(BF))
    place = (parts * SLOT, kmax)
    here = lax.broadcasted_iota(jnp.int32, place, 0) % SLOT == lax.broadcasted_iota(jnp.int32, place, 1)
    chosen = jnp.sum(jnp.where(here, spread_rows + 1.0, 0.0), axis=1, keepdims=True) - 1.0
    lane = lax.broadcasted_iota(jnp.int32, (parts * SLOT, n), 1).astype(F32)
    picks = jnp.where(chosen == lane, 1.0, 0.0)
    sm[...] = picks.astype(BF)
    st[...] = picks.T.astype(BF)
    dcat = dot_nt(grads[...], w_two[...])
    dcs[...] = dcat[:, :w]
    local, back_agg = trade_back(dcat[:, w:], k0, h0)
    dcs[...] += local

    wait(near_y)
    rows_near = trade_rows(owned(1).astype(BF), b1, t1)
    ft[zlow] = feats[:, :, near_cols].reshape(feat * n, half_cols).T
    wait(self_y)
    pself[...] = owned(0)
    wait(back_agg)
    dh[...] = dcs[...] + dot(st[...], h0[...])
    wait(rows_near)
    pre = pself[...] + dot(cm[...], t1[...]) * inv[...]
    sig = 1.0 / (1.0 + jnp.exp(-pre))
    d_pre = dh[...] * sig * (1.0 + pre * (1.0 - sig))
    chunks = 2 * w // TILE
    half = chunks // 2
    for k in range(half):
        dp[zlow, fi, k] = d_pre[:, k * TILE : (k + 1) * TILE].astype(BF)
    gathers = {}
    near_local, back_pre = trade_back(d_pre, k1, h1)
    dnl[...] = near_local
    for k in range(half):
        gathers[k] = gather_start(k)
    hidden = (pre * sig).astype(BF)
    joined[:, :w] = hidden
    rows_hidden = trade_rows(hidden, b2, t2)

    features_move.wait_recv()
    ft[1 - zlow] = fx[...].reshape(feat * n, half_cols).T
    wait(back_pre)
    d_near = (dnl[...] + dot(st[...], h1[...])).astype(BF)
    for k in range(half):
        dp[zlow, fi, half + k] = d_near[:, k * TILE : (k + 1) * TILE]
    for k in range(half, chunks):
        gathers[k] = gather_start(k)
    for k in range(half):
        gathers[k] = gather_forward(k, *gathers[k])

    wait(rows_hidden)
    agg = dot(cm[...], t2[...]) * inv[...]
    joined[:, w:] = agg.astype(BF)
    both = joined[...]
    out[0] = dot(both, w_two[...]).astype(BF)
    span = two.shape[0] // feat
    two_part = dot(both.T, grads[...]).astype(BF)
    for f in range(feat):
        ts[f % 2, (f // 2) * span : (f // 2 + 1) * span] = two_part[f * span : (f + 1) * span]
    two_core = send(ts.at[1 - c], u1, mate)

    for k in range(half, chunks):
        gathers[k] = gather_forward(k, *gathers[k])
    for k in range(half):
        gathers[k] = gather_end(k, *gathers[k])

    rows_x = half_cols // nx

    def chunk(k):
        g[k] = (
            dot(ft[0], dp[0, :, k].reshape(feat * n, TILE))
            + dot(ft[1], dp[1, :, k].reshape(feat * n, TILE))
        ).astype(BF)
        return [
            send(g.at[k, pl.ds(pl.multiple_of(t * rows_x, SLOT), rows_x)], rx.at[o, k],
                 (fi, z * nx + t))
            for o, t in enumerate(xpeers)
        ]

    def z_exchange(k, moves):
        wait(moves)
        total = g[k, pl.ds(pl.multiple_of(x * rows_x, SLOT), rows_x)].astype(F32)
        for o in range(nx - 1):
            total = total + rx[o, k].astype(F32)
        rz[zhigh, k] = total.astype(BF)
        part = rz.at[zhigh, k]
        return [send(part, part, (fi, t * nx + x)) for t in zpeers]

    def piece(k, low, at):
        return one.at[k, pl.ds(pl.multiple_of(low * half_cols + at * rows_x, SLOT), rows_x)]

    def first_gather(k, moves):
        wait(moves)
        total = rz[0, k].astype(F32)
        for o in range(1, nz // 2):
            total = total + rz[o, k].astype(F32)
        mine = piece(k, zlow, x)
        mine[...] = total.astype(BF)
        to_x = [send(mine, mine, (fi, z * nx + t)) for t in xpeers]
        return to_x, send(mine, mine, pair)

    def last_gather(k, moves):
        to_x, to_pair = moves
        rest = []
        if k % 2:
            to_pair.wait_recv()
            got = piece(k, 1 - zlow, x)
            rest = [send(got, got, (fi, z * nx + t)) for t in xpeers]
            return to_x + rest
        for o in range(1, nx):
            to_x[o - 1].wait_recv()
            got = piece(k, zlow, lax.rem(x - o + nx, nx))
            rest.append(send(got, got, pair))
        return [to_pair] + rest

    lanes_x = w // nx
    span_z = span // nz
    allz = [lax.rem(z + o, nz) for o in range(1, nz)]
    my_lanes = pl.ds(pl.multiple_of(x * lanes_x, 128), lanes_x)

    def two_y():
        two_core.wait_recv()
        ub[...] = (ts[c].astype(F32) + u1[...].astype(F32)).astype(BF)
        return [
            send(ub.at[pl.ds(pl.multiple_of(lax.rem(y + o, ny) * span, SLOT), span)],
                 u2.at[o - 1], ypeers[o - 1])
            for o in range(1, ny)
        ]

    def two_x(moves):
        wait(moves)
        total = ub[pl.ds(pl.multiple_of(y * span, SLOT), span)].astype(F32)
        for o in range(ny - 1):
            total = total + u2[o].astype(F32)
        for t in range(nx):
            v[t] = total[:, t * lanes_x : (t + 1) * lanes_x].astype(BF)
        return [send(v.at[t], vx.at[o], (fi, z * nx + t)) for o, t in enumerate(xpeers)]

    def two_z(moves):
        wait(moves)
        total = v[x].astype(F32)
        for o in range(nx - 1):
            total = total + vx[o].astype(F32)
        vs[...] = total.astype(BF)
        return [
            send(vs.at[pl.ds(pl.multiple_of(t * span_z, SLOT), span_z)], vz.at[o], (fi, t * nx + x))
            for o, t in enumerate(allz)
        ]

    def two_zg(moves):
        wait(moves)
        total = vs[pl.ds(pl.multiple_of(z * span_z, SLOT), span_z)].astype(F32)
        for o in range(nz - 1):
            total = total + vz[o].astype(F32)
        mine = pl.ds(pl.multiple_of(fi * span + z * span_z, SLOT), span_z)
        two[mine, my_lanes] = total.astype(BF)
        piece = two.at[mine, my_lanes]
        return [send(piece, piece, (fi, t * nx + x)) for t in allz]

    def two_xg(moves):
        wait(moves)
        piece = two.at[pl.ds(pl.multiple_of(fi * span, SLOT), span), my_lanes]
        return [send(piece, piece, (fi, z * nx + t)) for t in xpeers]

    def two_yg(moves):
        wait(moves)
        piece = two.at[pl.ds(pl.multiple_of(fi * span, SLOT), span)]
        return [send(piece, piece, device) for device in ypeers], send(piece, piece, mate)

    def two_across(moves):
        across = []
        for o in range(1, ny):
            moves[o - 1].wait_recv()
            source = lax.rem(y - o + ny, ny) * 2 + c
            piece = two.at[pl.ds(pl.multiple_of(source * span, SLOT), span)]
            across.append(send(piece, piece, mate))
        return across

    moves = {}
    marks = [len(copies)]
    drained = 0
    two_moves = two_y()
    for k in range(half):
        wait(gathers[k])
        moves[k] = chunk(k)
    for k in range(half, chunks):
        gathers[k] = gather_end(k, *gathers[k])
    for k in range(half, chunks):
        wait(gathers[k])
        moves[k] = chunk(k)
        moves[k - half] = z_exchange(k - half, moves[k - half])
    two_stages = [two_x, two_z, two_zg, two_xg]
    for step in range(1, chunks + 3):
        marks.append(len(copies))
        if half <= step < chunks:
            moves[step] = z_exchange(step, moves[step])
        if step >= 3:
            moves[step - 3] = last_gather(step - 3, moves[step - 3])
        if step <= chunks:
            moves[step - 1] = first_gather(step - 1, moves[step - 1])
        if step <= len(two_stages):
            two_moves = two_stages[step - 1](two_moves)
        elif step == len(two_stages) + 1:
            two_moves, two_mate = two_yg(two_moves)
        elif step == len(two_stages) + 2:
            two_moves = two_across(two_moves)
        settled = marks[max(step - 2, 0)]
        for copy in copies[drained:settled]:
            copy.wait_send()
        drained = settled
    for k in range(chunks):
        wait(moves[k])
    wait(two_moves)
    two_mate.wait_recv()
    for copy in copies[drained:]:
        copy.wait_send()


def finish(scale, out, one, two, out_hbm, one_hbm, two_hbm, one_wide, two_wide, sem):
    copies = [pltpu.make_async_copy(out, out_hbm, sem.at[0])]
    copies[0].start()
    for wide, target in ((one_wide, one_hbm), (two_wide, two_hbm)):
        rows = wide.shape[0] // 4
        for k in range(4):
            part = slice(k * rows, (k + 1) * rows)
            if wide is one_wide:
                for lane in range(one.shape[0]):
                    lanes = slice(lane * TILE, (lane + 1) * TILE)
                    wide[part, lanes] = one[lane, part].astype(F32) * scale
            else:
                wide[part] = two[part].astype(F32) * scale
            copy = pltpu.make_async_copy(wide.at[part], target.at[part], sem.at[len(copies)])
            copy.start()
            copies.append(copy)
    for copy in copies:
        copy.wait()


def on_device(nx, nz, features, w_one, w_two, neighbor, degree, send_rows, grad_out):
    feat, n, cols = features.shape
    w = w_two.shape[1]
    ny = feat // 2
    parts, kmax = send_rows.shape[1:]
    table = n + parts * SLOT
    edge = parts * SLOT
    half_cols = cols // 2
    rows_x = half_cols // nx
    span = 2 * w // feat
    lanes_x = w // nx
    chunks = 2 * w // TILE
    n_copies = (
        3 + 2 * (ny - 1) + 4 * (parts - 1)
        + chunks * (4 * ny + 2 + 4 * nx + nz)
        + 2 + 4 * ny + 2 * (nx + nz)
    )
    vm = pltpu.VMEM
    scratch = [
        vm(features.shape, BF), vm(w_one.shape, BF), vm(w_two.shape, BF),
        vm((neighbor.shape[2], 1, n), jnp.int32), vm((1, n), jnp.int32),
        vm((parts, kmax), jnp.int32), vm((n, w), BF),
        vm((2, 2, ny * n, w), F32), vm((2, 2, ny * n, w), BF), vm((2, ny * n, w), BF),
        vm((2, n, w), F32), vm((2, ny, n, w), BF), vm((2, ny - 1, n, w), BF),
        vm((n, table), BF), vm((table, n), BF), vm((edge, n), BF), vm((n, edge), BF),
        vm((table, w), BF), vm((table, w), BF), vm((edge, w), BF), vm((edge, w), BF),
        vm((edge, w), BF), vm((edge, w), BF), vm((edge, w), BF), vm((edge, w), BF),
        vm((n, 1), F32), vm((n, w), F32), vm((n, w), F32), vm((n, w), F32), vm((n, w), F32),
        vm((n, 2 * w), BF), vm((feat, n, half_cols), BF), vm((2, half_cols, feat * n), BF),
        vm((2, feat, chunks, n, TILE), BF),
        vm((chunks, half_cols, TILE), BF), vm((nx - 1, chunks, rows_x, TILE), BF),
        vm((nz // 2, chunks, rows_x, TILE), BF),
        vm((2, ny * span, w), BF), vm((ny * span, w), BF), vm((ny * span, w), BF),
        vm((ny - 1, span, w), BF), vm((nx, span, lanes_x), BF), vm((nx - 1, span, lanes_x), BF),
        vm((span, lanes_x), BF), vm((nz - 1, span // nz, lanes_x), BF),
        pltpu.SemaphoreType.DMA((n_copies,)), pltpu.SemaphoreType.DMA((n_copies,)),
        pltpu.SemaphoreType.DMA((8,)),
    ]
    spec = pl.BlockSpec(memory_space=pltpu.VMEM)
    hbm = pl.BlockSpec(memory_space=pltpu.HBM)
    out, one_sum, two_sum = pl.pallas_call(
        functools.partial(kernel, feat, nx, nz, kmax),
        out_shape=(
            jax.ShapeDtypeStruct((1, n, w), BF),
            jax.ShapeDtypeStruct((chunks, cols, TILE), BF),
            jax.ShapeDtypeStruct((2 * w, w), BF),
        ),
        in_specs=[hbm] * 7,
        out_specs=(spec, spec, spec),
        scratch_shapes=scratch,
        compiler_params=pltpu.CompilerParams(
            collective_id=0, has_side_effects=True, vmem_limit_bytes=40 * 1024 * 1024
        ),
    )(*(
        pltpu.with_memory_space_constraint(operand, pltpu.HBM)
        for operand in (
            features, w_one, w_two, jnp.transpose(neighbor, (2, 0, 1)), degree, send_rows[0],
            grad_out[0],
        )
    ))
    scale = 1.0 / math.sqrt(feat * n * parts)
    wide = (
        jax.ShapeDtypeStruct(out.shape, BF),
        jax.ShapeDtypeStruct((cols, 2 * w), F32),
        jax.ShapeDtypeStruct(two_sum.shape, F32),
    )
    return pl.pallas_call(
        functools.partial(finish, scale),
        out_shape=wide,
        in_specs=[spec] * 3,
        out_specs=(hbm, hbm, hbm),
        scratch_shapes=[
            vm((cols, 2 * w), F32), vm(two_sum.shape, F32), pltpu.SemaphoreType.DMA((9,)),
        ],
        compiler_params=pltpu.CompilerParams(vmem_limit_bytes=16 * 1024 * 1024),
    )(out, one_sum, two_sum)


def solution(mesh):
    parts = mesh.shape["dom"]
    nx = 1 << ((parts.bit_length() - 2) // 2)
    in_specs = (
        P(None, "dom", "feat"),
        P("feat", None),
        P(),
        P("feat", "dom", None),
        P("feat", "dom"),
        P("feat", "dom", None),
        P("feat", "dom", None),
    )
    out_specs = (P("feat", "dom", None), P("feat", None), P())
    return jax.shard_map(
        functools.partial(on_device, nx, parts // nx),
        mesh=mesh, in_specs=in_specs, out_specs=out_specs, check_vma=False,
    )
```

```python
import functools
import math

import jax
import jax.numpy as jnp
from jax import lax
from jax.experimental import pallas as pl
from jax.experimental.pallas import tpu as pltpu
from jax.sharding import PartitionSpec as P

BF = jnp.bfloat16
F32 = jnp.float32
SLOT = 16
TILE = 256


def dot(a, b):
    return jnp.dot(a, b, preferred_element_type=F32)


def dot_nt(a, b):
    return lax.dot_general(a, b, (((1,), (1,)), ((), ())), preferred_element_type=F32)


def kernel(
    feat, nx, nz, kmax,
    feats_hbm, w_one_hbm, w_two_hbm, nbr_hbm, deg_hbm, sends_hbm, grads_hbm,
    out, one, two,
    feats, w_one, w_two, nbr, deg, sends, grads,
    proj, projb, r1, q, qb, r2, cm, ct, sm, st, t1, t2, b1, b2, k0, k1, h0, h1,
    inv, dcs, dh, pself, dnl, joined, fx, ft, dp, g, rx, rz, ts, u1, ub, u2, v, vx, vs, vz,
    ssem, rsem, lsem,
):
    ny = feat // 2
    parts = nx * nz
    n = nbr.shape[2]
    w = grads.shape[1]
    cols = w_one.shape[0]
    fan = nbr.shape[0]
    half_cols = cols // 2
    fi = lax.axis_index("feat")
    di = lax.axis_index("dom")
    y, c = fi // 2, fi % 2
    z, x = di // nx, di % nx
    mate = (y * 2 + 1 - c, di)
    zlow, zhigh = z % 2, z // 2
    pair = (fi, (z + 1 - 2 * zlow) * nx + x)
    count = [0]

    def send(src, dst, device):
        k = count[0]
        count[0] += 1
        copy = pltpu.make_async_remote_copy(
            src_ref=src, dst_ref=dst, send_sem=ssem.at[k], recv_sem=rsem.at[k],
            device_id=device, device_id_type=pl.DeviceIdType.MESH,
        )
        copy.start()
        copies.append(copy)
        return copy

    copies = []
    ypeers = [(lax.rem(y + o, ny) * 2 + c, di) for o in range(1, ny)]
    dpeers = [lax.rem(di + o, parts) for o in range(1, parts)]
    xpeers = [lax.rem(x + o, nx) for o in range(1, nx)]
    zpeers = [lax.rem(zhigh + o, nz // 2) * 2 + zlow for o in range(1, nz // 2)]

    barrier = pltpu.get_barrier_semaphore()
    everyone = [mate] + ypeers + [(fi, p) for p in dpeers]
    for device in everyone:
        pl.semaphore_signal(barrier, inc=1, device_id=device, device_id_type=pl.DeviceIdType.MESH)

    def load(k, src, dst):
        copy = pltpu.make_async_copy(src, dst, lsem.at[k])
        copy.start()
        return copy

    first_loads = [load(0, w_one_hbm.at[:, w:], w_one.at[:, w:]), load(1, feats_hbm, feats)]
    self_load = load(2, w_one_hbm.at[:, :w], w_one.at[:, :w])
    later_loads = [
        load(3, nbr_hbm, nbr), load(4, deg_hbm, deg), load(5, sends_hbm, sends),
        load(6, grads_hbm, grads), load(7, w_two_hbm, w_two),
    ]

    def project(h):
        flat = feats[...].reshape(feat * n, cols)
        for t in range(w // TILE):
            acc = dot(flat, w_one[:, h * w + t * TILE : h * w + (t + 1) * TILE])
            for f in range(feat):
                part = acc[f * n : (f + 1) * n]
                rows = slice((f // 2) * n, (f // 2 + 1) * n)
                lanes = slice(t * TILE, (t + 1) * TILE)
                proj[h, f % 2, rows, lanes] = part
                projb[h, f % 2, rows, lanes] = part.astype(BF)

    def core_send(h):
        return send(projb.at[h, 1 - c], r1.at[h], mate)

    def y_send(h):
        for j in range(ny):
            rows = slice(j * n, (j + 1) * n)
            qb[h, j] = (proj[h, c, rows] + r1[h, rows].astype(F32)).astype(BF)
        mine = pl.ds(pl.multiple_of(y * n, n), n)
        q[h] = proj[h, c, mine] + r1[h, mine].astype(F32)
        return [
            send(qb.at[h, lax.rem(y + o, ny)], r2.at[h, o - 1], ypeers[o - 1])
            for o in range(1, ny)
        ]

    def owned(h):
        total = q[h]
        for o in range(ny - 1):
            total = total + r2[h, o].astype(F32)
        return total

    def wait(items):
        for item in items:
            item.wait_recv()

    def slot(p):
        return pl.ds(pl.multiple_of(p * SLOT, SLOT), SLOT)

    def table_slot(p):
        return pl.ds(pl.multiple_of(n + p * SLOT, SLOT), SLOT)

    def trade_rows(values, boxes, table):
        table[:n] = values
        boxes[...] = dot(sm[...], values).astype(BF)
        table[table_slot(di)] = boxes[slot(di)]
        return [send(boxes.at[slot(p)], table.at[table_slot(di)], (fi, p)) for p in dpeers]

    def trade_back(values, outgoing, returned):
        terms = dot(ct[...], (values * inv[...]).astype(BF))
        outgoing[...] = terms[n:].astype(BF)
        returned[slot(di)] = outgoing[slot(di)]
        moves = [send(outgoing.at[slot(p)], returned.at[slot(di)], (fi, p)) for p in dpeers]
        return terms[:n], moves

    def pass_on(low, f, k, device):
        block = dp.at[low, f, k]
        return send(block, block, device)

    def y_source(o):
        return lax.rem(y - o + ny, ny) * 2 + c

    def gather_start(k):
        to_pair = pass_on(zlow, fi, k, pair)
        to_y = [pass_on(zlow, fi, k, device) for device in ypeers]
        return [to_pair], to_y, [pass_on(zlow, fi, k, mate)]

    def gather_forward(k, to_pair, to_y, to_mate):
        if k % 2:
            to_pair[0].wait_recv()
            far = [pass_on(1 - zlow, fi, k, device) for device in ypeers]
            to_mate.append(pass_on(1 - zlow, fi, k, mate))
            return far, to_y, to_mate
        for o in range(1, ny):
            to_y[o - 1].wait_recv()
            to_pair.append(pass_on(zlow, y_source(o), k, pair))
            to_mate.append(pass_on(zlow, y_source(o), k, mate))
        return to_pair, to_y, to_mate

    def gather_end(k, later, to_y, to_mate):
        if k % 2:
            for low, moves in ((zlow, to_y), (1 - zlow, later)):
                for o in range(1, ny):
                    moves[o - 1].wait_recv()
                    to_mate.append(pass_on(low, y_source(o), k, mate))
            return to_mate
        for o in range(ny):
            later[o].wait_recv()
            to_mate.append(pass_on(1 - zlow, y_source(o), k, mate))
        return to_mate

    first_loads[1].wait()
    pl.semaphore_wait(barrier, len(everyone))
    far_cols = pl.ds(pl.multiple_of((1 - zlow) * half_cols, 128), half_cols)
    near_cols = pl.ds(pl.multiple_of(zlow * half_cols, 128), half_cols)
    def send_features(f):
        return send(feats.at[f, :, far_cols], fx.at[f], pair)

    features_moves = [send_features(f) for f in range(feat // 2)]
    first_loads[0].wait()
    project(1)
    near_core = core_send(1)
    self_load.wait()
    project(0)
    self_core = core_send(0)
    near_core.wait_recv()
    near_y = y_send(1)
    self_core.wait_recv()
    self_y = y_send(0)

    for item in later_loads:
        item.wait()
    eye = lax.broadcasted_iota(jnp.int32, (n, n), 0) == lax.broadcasted_iota(jnp.int32, (n, n), 1)
    inv[...] = 1.0 / jnp.sum(jnp.where(eye, deg[...].astype(F32), 0.0), axis=1, keepdims=True)
    entry = lax.broadcasted_iota(jnp.int32, (n + parts * SLOT, n), 0)
    extra = entry - n
    code = jnp.where(
        entry < n, entry,
        jnp.where((extra & 15) < kmax, n + (extra >> 4) * kmax + (extra & 15), -2),
    )
    counts = jnp.zeros(code.shape, F32)
    for s in range(fan):
        used = jnp.where(s < deg[...], nbr[s], -1)
        counts = counts + jnp.where(used == code, 1.0, 0.0)
    ct[...] = counts.astype(BF)
    cm[...] = counts.T.astype(BF)
    edge = (parts * SLOT, parts)
    owner = lax.broadcasted_iota(jnp.int32, edge, 0) >> 4 == lax.broadcasted_iota(jnp.int32, edge, 1)
    spread_rows = dot(jnp.where(owner, 1.0, 0.0).astype(BF), sends[...].astype(F32).astype(BF))
    place = (parts * SLOT, kmax)
    here = lax.broadcasted_iota(jnp.int32, place, 0) & 15 == lax.broadcasted_iota(jnp.int32, place, 1)
    chosen = jnp.sum(jnp.where(here, spread_rows + 1.0, 0.0), axis=1, keepdims=True) - 1.0
    lane = lax.broadcasted_iota(jnp.int32, (parts * SLOT, n), 1).astype(F32)
    picks = jnp.where(chosen == lane, 1.0, 0.0)
    sm[...] = picks.astype(BF)
    st[...] = picks.T.astype(BF)
    dcat = dot_nt(grads[...], w_two[...])
    dcs[...] = dcat[:, :w]
    local, back_agg = trade_back(dcat[:, w:], k0, h0)
    dcs[...] += local

    wait(near_y)
    rows_near = trade_rows(owned(1).astype(BF), b1, t1)
    features_moves += [send_features(f) for f in range(feat // 2, feat)]
    ft[zlow] = feats[:, :, near_cols].reshape(feat * n, half_cols).T
    wait(self_y)
    pself[...] = owned(0)
    wait(back_agg)
    dh[...] = dcs[...] + dot(st[...], h0[...])
    wait(rows_near)
    pre = pself[...] + dot(cm[...], t1[...]) * inv[...]
    sig = 1.0 / (1.0 + jnp.exp(-pre))
    d_pre = dh[...] * sig * (1.0 + pre * (1.0 - sig))
    chunks = 2 * w // TILE
    half = chunks // 2
    for k in range(half):
        dp[zlow, fi, k] = d_pre[:, k * TILE : (k + 1) * TILE].astype(BF)
    gathers = {}
    near_local, back_pre = trade_back(d_pre, k1, h1)
    dnl[...] = near_local
    for k in range(half):
        gathers[k] = gather_start(k)
    hidden = (pre * sig).astype(BF)
    joined[:, :w] = hidden
    rows_hidden = trade_rows(hidden, b2, t2)

    wait(features_moves)
    ft[1 - zlow] = fx[...].reshape(feat * n, half_cols).T
    wait(back_pre)
    d_near = (dnl[...] + dot(st[...], h1[...])).astype(BF)
    for k in range(half):
        dp[zlow, fi, half + k] = d_near[:, k * TILE : (k + 1) * TILE]
    for k in range(half, chunks):
        gathers[k] = gather_start(k)
    for k in range(half):
        gathers[k] = gather_forward(k, *gathers[k])

    for k in range(half, chunks):
        gathers[k] = gather_forward(k, *gathers[k])
    for k in range(half):
        gathers[k] = gather_end(k, *gathers[k])

    rows_x = half_cols // nx

    def chunk(k):
        g[k] = (
            dot(ft[0], dp[0, :, k].reshape(feat * n, TILE))
            + dot(ft[1], dp[1, :, k].reshape(feat * n, TILE))
        ).astype(BF)
        return [
            send(g.at[k, pl.ds(pl.multiple_of(t * rows_x, SLOT), rows_x)], rx.at[o, k],
                 (fi, z * nx + t))
            for o, t in enumerate(xpeers)
        ]

    def z_exchange(k, moves):
        wait(moves)
        total = g[k, pl.ds(pl.multiple_of(x * rows_x, SLOT), rows_x)].astype(F32)
        for o in range(nx - 1):
            total = total + rx[o, k].astype(F32)
        rz[zhigh, k] = total.astype(BF)
        part = rz.at[zhigh, k]
        return [send(part, part, (fi, t * nx + x)) for t in zpeers]

    def piece(k, low, at):
        return one.at[k, pl.ds(pl.multiple_of(low * half_cols + at * rows_x, SLOT), rows_x)]

    def first_gather(k, moves):
        wait(moves)
        total = rz[0, k].astype(F32)
        for o in range(1, nz // 2):
            total = total + rz[o, k].astype(F32)
        mine = piece(k, zlow, x)
        mine[...] = total.astype(BF)
        to_x = [send(mine, mine, (fi, z * nx + t)) for t in xpeers]
        return to_x, send(mine, mine, pair)

    def last_gather(k, moves):
        to_x, to_pair = moves
        rest = []
        if k % 2:
            to_pair.wait_recv()
            got = piece(k, 1 - zlow, x)
            rest = [send(got, got, (fi, z * nx + t)) for t in xpeers]
            return to_x + rest
        for o in range(1, nx):
            to_x[o - 1].wait_recv()
            got = piece(k, zlow, lax.rem(x - o + nx, nx))
            rest.append(send(got, got, pair))
        return [to_pair] + rest

    span = two.shape[0] // feat
    lanes_x = w // nx
    span_z = span // nz
    allz = [lax.rem(z + o, nz) for o in range(1, nz)]
    my_lanes = pl.ds(pl.multiple_of(x * lanes_x, 128), lanes_x)

    def layer_two():
        wait(rows_hidden)
        agg = dot(cm[...], t2[...]) * inv[...]
        joined[:, w:] = agg.astype(BF)
        both = joined[...]
        out[0] = dot(both, w_two[...]).astype(BF)
        two_part = dot(both.T, grads[...]).astype(BF)
        for f in range(feat):
            ts[f % 2, (f // 2) * span : (f // 2 + 1) * span] = two_part[f * span : (f + 1) * span]
        return send(ts.at[1 - c], u1, mate)

    def two_y(two_core):
        two_core.wait_recv()
        ub[...] = (ts[c].astype(F32) + u1[...].astype(F32)).astype(BF)
        return [
            send(ub.at[pl.ds(pl.multiple_of(lax.rem(y + o, ny) * span, SLOT), span)],
                 u2.at[o - 1], ypeers[o - 1])
            for o in range(1, ny)
        ]

    def two_x(moves):
        wait(moves)
        total = ub[pl.ds(pl.multiple_of(y * span, SLOT), span)].astype(F32)
        for o in range(ny - 1):
            total = total + u2[o].astype(F32)
        for t in range(nx):
            v[t] = total[:, t * lanes_x : (t + 1) * lanes_x].astype(BF)
        return [send(v.at[t], vx.at[o], (fi, z * nx + t)) for o, t in enumerate(xpeers)]

    def two_z(moves):
        wait(moves)
        total = v[x].astype(F32)
        for o in range(nx - 1):
            total = total + vx[o].astype(F32)
        vs[...] = total.astype(BF)
        return [
            send(vs.at[pl.ds(pl.multiple_of(t * span_z, SLOT), span_z)], vz.at[o], (fi, t * nx + x))
            for o, t in enumerate(allz)
        ]

    def two_zg(moves):
        wait(moves)
        total = vs[pl.ds(pl.multiple_of(z * span_z, SLOT), span_z)].astype(F32)
        for o in range(nz - 1):
            total = total + vz[o].astype(F32)
        mine = pl.ds(pl.multiple_of(fi * span + z * span_z, SLOT), span_z)
        two[mine, my_lanes] = total.astype(BF)
        piece = two.at[mine, my_lanes]
        return [send(piece, piece, (fi, t * nx + x)) for t in allz]

    def two_xg(moves):
        wait(moves)
        piece = two.at[pl.ds(pl.multiple_of(fi * span, SLOT), span), my_lanes]
        return [send(piece, piece, (fi, z * nx + t)) for t in xpeers]

    def two_yg(moves):
        wait(moves)
        piece = two.at[pl.ds(pl.multiple_of(fi * span, SLOT), span)]
        return [send(piece, piece, device) for device in ypeers], send(piece, piece, mate)

    def two_across(moves):
        across = []
        for o in range(1, ny):
            moves[o - 1].wait_recv()
            source = lax.rem(y - o + ny, ny) * 2 + c
            piece = two.at[pl.ds(pl.multiple_of(source * span, SLOT), span)]
            across.append(send(piece, piece, mate))
        return across

    moves = {}
    marks = [len(copies)]
    drained = 0
    for k in range(half):
        wait(gathers[k])
        moves[k] = chunk(k)
    two_core = layer_two()
    for k in range(half, chunks):
        gathers[k] = gather_end(k, *gathers[k])
    for k in range(half, chunks):
        wait(gathers[k])
        moves[k] = chunk(k)
        moves[k - half] = z_exchange(k - half, moves[k - half])
    two_moves = two_y(two_core)
    two_stages = [two_x, two_z, two_zg, two_xg]
    for step in range(1, chunks + 3):
        marks.append(len(copies))
        if half <= step < chunks:
            moves[step] = z_exchange(step, moves[step])
        if step >= 3:
            moves[step - 3] = last_gather(step - 3, moves[step - 3])
        if step <= chunks:
            moves[step - 1] = first_gather(step - 1, moves[step - 1])
        if step <= len(two_stages):
            two_moves = two_stages[step - 1](two_moves)
        elif step == len(two_stages) + 1:
            two_moves, two_mate = two_yg(two_moves)
        elif step == len(two_stages) + 2:
            two_moves = two_across(two_moves)
        settled = marks[max(step - 2, 0)]
        for copy in copies[drained:settled]:
            copy.wait_send()
        drained = settled
    for k in range(chunks):
        wait(moves[k])
    wait(two_moves)
    two_mate.wait_recv()
    for copy in copies[drained:]:
        copy.wait_send()


def finish(scale, out, one, two, out_hbm, one_hbm, two_hbm, one_wide, two_wide, sem):
    copies = [pltpu.make_async_copy(out, out_hbm, sem.at[0])]
    copies[0].start()
    for wide, target in ((one_wide, one_hbm), (two_wide, two_hbm)):
        rows = wide.shape[0] // 4
        for k in range(4):
            part = slice(k * rows, (k + 1) * rows)
            if wide is one_wide:
                for lane in range(one.shape[0]):
                    lanes = slice(lane * TILE, (lane + 1) * TILE)
                    wide[part, lanes] = one[lane, part].astype(F32) * scale
            else:
                wide[part] = two[part].astype(F32) * scale
            copy = pltpu.make_async_copy(wide.at[part], target.at[part], sem.at[len(copies)])
            copy.start()
            copies.append(copy)
    for copy in copies:
        copy.wait()


def on_device(nx, nz, features, w_one, w_two, neighbor, degree, send_rows, grad_out):
    feat, n, cols = features.shape
    w = w_two.shape[1]
    ny = feat // 2
    parts, kmax = send_rows.shape[1:]
    table = n + parts * SLOT
    edge = parts * SLOT
    half_cols = cols // 2
    rows_x = half_cols // nx
    span = 2 * w // feat
    lanes_x = w // nx
    chunks = 2 * w // TILE
    n_copies = (
        2 + feat + 2 * (ny - 1) + 4 * (parts - 1)
        + chunks * (4 * ny + 2 + 4 * nx + nz)
        + 2 + 4 * ny + 2 * (nx + nz)
    )
    vm = pltpu.VMEM
    scratch = [
        vm(features.shape, BF), vm(w_one.shape, BF), vm(w_two.shape, BF),
        vm((neighbor.shape[2], 1, n), jnp.int32), vm((1, n), jnp.int32),
        vm((parts, kmax), jnp.int32), vm((n, w), BF),
        vm((2, 2, ny * n, w), F32), vm((2, 2, ny * n, w), BF), vm((2, ny * n, w), BF),
        vm((2, n, w), F32), vm((2, ny, n, w), BF), vm((2, ny - 1, n, w), BF),
        vm((n, table), BF), vm((table, n), BF), vm((edge, n), BF), vm((n, edge), BF),
        vm((table, w), BF), vm((table, w), BF), vm((edge, w), BF), vm((edge, w), BF),
        vm((edge, w), BF), vm((edge, w), BF), vm((edge, w), BF), vm((edge, w), BF),
        vm((n, 1), F32), vm((n, w), F32), vm((n, w), F32), vm((n, w), F32), vm((n, w), F32),
        vm((n, 2 * w), BF), vm((feat, n, half_cols), BF), vm((2, half_cols, feat * n), BF),
        vm((2, feat, chunks, n, TILE), BF),
        vm((chunks, half_cols, TILE), BF), vm((nx - 1, chunks, rows_x, TILE), BF),
        vm((nz // 2, chunks, rows_x, TILE), BF),
        vm((2, ny * span, w), BF), vm((ny * span, w), BF), vm((ny * span, w), BF),
        vm((ny - 1, span, w), BF), vm((nx, span, lanes_x), BF), vm((nx - 1, span, lanes_x), BF),
        vm((span, lanes_x), BF), vm((nz - 1, span // nz, lanes_x), BF),
        pltpu.SemaphoreType.DMA((n_copies,)), pltpu.SemaphoreType.DMA((n_copies,)),
        pltpu.SemaphoreType.DMA((8,)),
    ]
    spec = pl.BlockSpec(memory_space=pltpu.VMEM)
    hbm = pl.BlockSpec(memory_space=pltpu.HBM)
    out, one_sum, two_sum = pl.pallas_call(
        functools.partial(kernel, feat, nx, nz, kmax),
        out_shape=(
            jax.ShapeDtypeStruct((1, n, w), BF),
            jax.ShapeDtypeStruct((chunks, cols, TILE), BF),
            jax.ShapeDtypeStruct((2 * w, w), BF),
        ),
        in_specs=[hbm] * 7,
        out_specs=(spec, spec, spec),
        scratch_shapes=scratch,
        compiler_params=pltpu.CompilerParams(
            collective_id=0, has_side_effects=True, vmem_limit_bytes=40 * 1024 * 1024
        ),
    )(*(
        pltpu.with_memory_space_constraint(operand, pltpu.HBM)
        for operand in (
            features, w_one, w_two, jnp.transpose(neighbor, (2, 0, 1)), degree, send_rows[0],
            grad_out[0],
        )
    ))
    scale = 1.0 / math.sqrt(feat * n * parts)
    wide = (
        jax.ShapeDtypeStruct(out.shape, BF),
        jax.ShapeDtypeStruct((cols, 2 * w), F32),
        jax.ShapeDtypeStruct(two_sum.shape, F32),
    )
    return pl.pallas_call(
        functools.partial(finish, scale),
        out_shape=wide,
        in_specs=[spec] * 3,
        out_specs=(hbm, hbm, hbm),
        scratch_shapes=[
            vm((cols, 2 * w), F32), vm(two_sum.shape, F32), pltpu.SemaphoreType.DMA((9,)),
        ],
        compiler_params=pltpu.CompilerParams(vmem_limit_bytes=16 * 1024 * 1024),
    )(out, one_sum, two_sum)


def solution(mesh):
    parts = mesh.shape["dom"]
    nx = 1 << ((parts.bit_length() - 2) // 2)
    in_specs = (
        P(None, "dom", "feat"),
        P("feat", None),
        P(),
        P("feat", "dom", None),
        P("feat", "dom"),
        P("feat", "dom", None),
        P("feat", "dom", None),
    )
    out_specs = (P("feat", "dom", None), P("feat", None), P())
    return jax.shard_map(
        functools.partial(on_device, nx, parts // nx),
        mesh=mesh, in_specs=in_specs, out_specs=out_specs, check_vma=False,
    )
```

```python
import functools
import math

import jax
import jax.numpy as jnp
from jax import lax
from jax.experimental import pallas as pl
from jax.experimental.pallas import tpu as pltpu
from jax.sharding import PartitionSpec as P

BF = jnp.bfloat16
F32 = jnp.float32
SLOT = 16
TILE = 256


def dot(a, b):
    return jnp.dot(a, b, preferred_element_type=F32)


def dot_nt(a, b):
    return lax.dot_general(a, b, (((1,), (1,)), ((), ())), preferred_element_type=F32)


def kernel(
    feat, nx, nz, kmax,
    feats_hbm, w_one_hbm, w_two_hbm, nbr_hbm, deg_hbm, sends_hbm, grads_hbm,
    out, one, two,
    feats, w_one, w_two, nbr, deg, sends, grads,
    proj, projb, r1, q, qb, r2, cm, ct, cf, cft, sm, st, t1, t2, b1, b2, k0, k1, h0, h1,
    inv, dcs, dh, pself, dnl, joined, fx, ft, dp, g, rx, rz, ts, u1, ub, u2, v, vx, vs, vz,
    ssem, rsem, lsem,
):
    ny = feat // 2
    parts = nx * nz
    n = nbr.shape[2]
    w = grads.shape[1]
    cols = w_one.shape[0]
    fan = nbr.shape[0]
    half_cols = cols // 2
    fi = lax.axis_index("feat")
    di = lax.axis_index("dom")
    y, c = fi // 2, fi % 2
    z, x = di // nx, di % nx
    mate = (y * 2 + 1 - c, di)
    zlow, zhigh = z % 2, z // 2
    pair = (fi, (z + 1 - 2 * zlow) * nx + x)
    count = [0]

    def send(src, dst, device):
        k = count[0]
        count[0] += 1
        copy = pltpu.make_async_remote_copy(
            src_ref=src, dst_ref=dst, send_sem=ssem.at[k], recv_sem=rsem.at[k],
            device_id=device, device_id_type=pl.DeviceIdType.MESH,
        )
        copy.start()
        copies.append(copy)
        return copy

    copies = []
    ypeers = [(lax.rem(y + o, ny) * 2 + c, di) for o in range(1, ny)]
    dpeers = [lax.rem(di + o, parts) for o in range(1, parts)]
    xpeers = [lax.rem(x + o, nx) for o in range(1, nx)]
    zpeers = [lax.rem(zhigh + o, nz // 2) * 2 + zlow for o in range(1, nz // 2)]

    barrier = pltpu.get_barrier_semaphore()
    everyone = [mate] + ypeers + [(fi, p) for p in dpeers]
    for device in everyone:
        pl.semaphore_signal(barrier, inc=1, device_id=device, device_id_type=pl.DeviceIdType.MESH)

    def load(k, src, dst):
        copy = pltpu.make_async_copy(src, dst, lsem.at[k])
        copy.start()
        return copy

    first_loads = [load(0, w_one_hbm.at[:, w:], w_one.at[:, w:]), load(1, feats_hbm, feats)]
    self_load = load(2, w_one_hbm.at[:, :w], w_one.at[:, :w])
    later_loads = [
        load(3, nbr_hbm, nbr), load(4, deg_hbm, deg), load(5, sends_hbm, sends),
        load(6, grads_hbm, grads), load(7, w_two_hbm, w_two),
    ]

    def project(h):
        flat = feats[...].reshape(feat * n, cols)
        for t in range(w // TILE):
            acc = dot(flat, w_one[:, h * w + t * TILE : h * w + (t + 1) * TILE])
            for f in range(feat):
                part = acc[f * n : (f + 1) * n]
                rows = slice((f // 2) * n, (f // 2 + 1) * n)
                lanes = slice(t * TILE, (t + 1) * TILE)
                proj[h, f % 2, rows, lanes] = part
                projb[h, f % 2, rows, lanes] = part.astype(BF)

    def core_send(h):
        return send(projb.at[h, 1 - c], r1.at[h], mate)

    def y_send(h):
        for j in range(ny):
            rows = slice(j * n, (j + 1) * n)
            qb[h, j] = (proj[h, c, rows] + r1[h, rows].astype(F32)).astype(BF)
        mine = pl.ds(pl.multiple_of(y * n, n), n)
        q[h] = proj[h, c, mine] + r1[h, mine].astype(F32)
        return [
            send(qb.at[h, lax.rem(y + o, ny)], r2.at[h, o - 1], ypeers[o - 1])
            for o in range(1, ny)
        ]

    def owned(h):
        total = q[h]
        for o in range(ny - 1):
            total = total + r2[h, o].astype(F32)
        return total

    def wait(items):
        for item in items:
            item.wait_recv()

    def slot(p):
        return pl.ds(pl.multiple_of(p * SLOT, SLOT), SLOT)

    wide = w // 2

    def trade_rows(values, boxes, table):
        boxes[...] = (dot(sm[0], values[:, :wide]) + dot(sm[1], values[:, wide:])).astype(BF)
        table[slot(di)] = boxes[slot(di)]
        return [send(boxes.at[slot(p)], table.at[slot(di)], (fi, p)) for p in dpeers]

    def table_mean(values, table):
        rows = table[...]
        far = jnp.concatenate([dot(cf[0], rows), dot(cf[1], rows)], axis=1)
        return (dot(cm[...], values) + far) * inv[...]

    def trade_back(values, outgoing, returned):
        scaled = (values * inv[...]).astype(BF)
        outgoing[...] = (
            dot(cft[0], scaled[:, :wide]) + dot(cft[1], scaled[:, wide:])
        ).astype(BF)
        returned[slot(di)] = outgoing[slot(di)]
        moves = [send(outgoing.at[slot(p)], returned.at[slot(di)], (fi, p)) for p in dpeers]
        return dot(ct[...], scaled), moves

    def come_home(returned):
        rows = returned[...]
        return jnp.concatenate([dot(st[0], rows), dot(st[1], rows)], axis=1)

    def pass_on(low, f, k, device):
        block = dp.at[low, f, k]
        return send(block, block, device)

    def y_source(o):
        return lax.rem(y - o + ny, ny) * 2 + c

    def gather_start(k):
        to_pair = pass_on(zlow, fi, k, pair)
        to_y = [pass_on(zlow, fi, k, device) for device in ypeers]
        return [to_pair], to_y, [pass_on(zlow, fi, k, mate)]

    def gather_forward(k, to_pair, to_y, to_mate):
        if k % 2:
            to_pair[0].wait_recv()
            far = [pass_on(1 - zlow, fi, k, device) for device in ypeers]
            to_mate.append(pass_on(1 - zlow, fi, k, mate))
            return far, to_y, to_mate
        for o in range(1, ny):
            to_y[o - 1].wait_recv()
            to_pair.append(pass_on(zlow, y_source(o), k, pair))
            to_mate.append(pass_on(zlow, y_source(o), k, mate))
        return to_pair, to_y, to_mate

    def gather_end(k, later, to_y, to_mate):
        if k % 2:
            for low, moves in ((zlow, to_y), (1 - zlow, later)):
                for o in range(1, ny):
                    moves[o - 1].wait_recv()
                    to_mate.append(pass_on(low, y_source(o), k, mate))
            return to_mate
        for o in range(ny):
            later[o].wait_recv()
            to_mate.append(pass_on(1 - zlow, y_source(o), k, mate))
        return to_mate

    first_loads[1].wait()
    pl.semaphore_wait(barrier, len(everyone))
    far_cols = pl.ds(pl.multiple_of((1 - zlow) * half_cols, 128), half_cols)
    near_cols = pl.ds(pl.multiple_of(zlow * half_cols, 128), half_cols)
    def send_features(f):
        return send(feats.at[f, :, far_cols], fx.at[f], pair)

    features_moves = [send_features(f) for f in range(feat // 2)]
    first_loads[0].wait()
    project(1)
    near_core = core_send(1)
    self_load.wait()
    project(0)
    self_core = core_send(0)
    near_core.wait_recv()
    near_y = y_send(1)
    self_core.wait_recv()
    self_y = y_send(0)

    for item in later_loads:
        item.wait()
    eye = lax.broadcasted_iota(jnp.int32, (n, n), 0) == lax.broadcasted_iota(jnp.int32, (n, n), 1)
    inv[...] = 1.0 / jnp.sum(jnp.where(eye, deg[...].astype(F32), 0.0), axis=1, keepdims=True)
    def tally(code):
        total = jnp.zeros(code.shape, F32)
        for s in range(fan):
            used = jnp.where(s < deg[...], nbr[s], -1)
            total = total + jnp.where(used == code, 1.0, 0.0)
        return total

    own = tally(lax.broadcasted_iota(jnp.int32, (n, n), 0))
    ct[...] = own.astype(BF)
    cm[...] = own.T.astype(BF)
    entry = lax.broadcasted_iota(jnp.int32, (parts * SLOT, n), 0)
    for h in range(2):
        k = (entry & 15) - h * kmax
        far = tally(jnp.where((k >= 0) & (k < kmax), n + (entry >> 4) * kmax + k, -2))
        cft[h] = far.astype(BF)
        cf[h] = far.T.astype(BF)
    edge = (parts * SLOT, parts)
    owner = lax.broadcasted_iota(jnp.int32, edge, 0) >> 4 == lax.broadcasted_iota(jnp.int32, edge, 1)
    spread_rows = dot(jnp.where(owner, 1.0, 0.0).astype(BF), sends[...].astype(F32).astype(BF))
    place = (parts * SLOT, kmax)
    spot = lax.broadcasted_iota(jnp.int32, place, 0) & 15
    lane = lax.broadcasted_iota(jnp.int32, (parts * SLOT, n), 1).astype(F32)
    for h in range(2):
        here = spot == lax.broadcasted_iota(jnp.int32, place, 1) + h * kmax
        chosen = jnp.sum(jnp.where(here, spread_rows + 1.0, 0.0), axis=1, keepdims=True) - 1.0
        picks = jnp.where(chosen == lane, 1.0, 0.0)
        sm[h] = picks.astype(BF)
        st[h] = picks.T.astype(BF)
    dcat = dot_nt(grads[...], w_two[...])
    dcs[...] = dcat[:, :w]
    local, back_agg = trade_back(dcat[:, w:], k0, h0)
    dcs[...] += local

    wait(near_y)
    p_near = owned(1).astype(BF)
    rows_near = trade_rows(p_near, b1, t1)
    features_moves += [send_features(f) for f in range(feat // 2, feat)]
    ft[zlow] = feats[:, :, near_cols].reshape(feat * n, half_cols).T
    wait(self_y)
    pself[...] = owned(0)
    wait(back_agg)
    dh[...] = dcs[...] + come_home(h0)
    wait(rows_near)
    pre = pself[...] + table_mean(p_near, t1)
    sig = 1.0 / (1.0 + jnp.exp(-pre))
    d_pre = dh[...] * sig * (1.0 + pre * (1.0 - sig))
    chunks = 2 * w // TILE
    half = chunks // 2
    for k in range(half):
        dp[zlow, fi, k] = d_pre[:, k * TILE : (k + 1) * TILE].astype(BF)
    gathers = {}
    near_local, back_pre = trade_back(d_pre, k1, h1)
    dnl[...] = near_local
    for k in range(half):
        gathers[k] = gather_start(k)
    hidden = (pre * sig).astype(BF)
    joined[:, :w] = hidden
    rows_hidden = trade_rows(hidden, b2, t2)

    wait(features_moves)
    ft[1 - zlow] = fx[...].reshape(feat * n, half_cols).T
    wait(back_pre)
    d_near = (dnl[...] + come_home(h1)).astype(BF)
    for k in range(half):
        dp[zlow, fi, half + k] = d_near[:, k * TILE : (k + 1) * TILE]
    for k in range(half, chunks):
        gathers[k] = gather_start(k)
    for k in range(half):
        gathers[k] = gather_forward(k, *gathers[k])

    for k in range(half, chunks):
        gathers[k] = gather_forward(k, *gathers[k])
    for k in range(half):
        gathers[k] = gather_end(k, *gathers[k])

    rows_x = half_cols // nx

    def chunk(k):
        g[k] = (
            dot(ft[0], dp[0, :, k].reshape(feat * n, TILE))
            + dot(ft[1], dp[1, :, k].reshape(feat * n, TILE))
        ).astype(BF)
        return [
            send(g.at[k, pl.ds(pl.multiple_of(t * rows_x, SLOT), rows_x)], rx.at[o, k],
                 (fi, z * nx + t))
            for o, t in enumerate(xpeers)
        ]

    def z_exchange(k, moves):
        wait(moves)
        total = g[k, pl.ds(pl.multiple_of(x * rows_x, SLOT), rows_x)].astype(F32)
        for o in range(nx - 1):
            total = total + rx[o, k].astype(F32)
        rz[zhigh, k] = total.astype(BF)
        part = rz.at[zhigh, k]
        return [send(part, part, (fi, t * nx + x)) for t in zpeers]

    def piece(k, low, at):
        return one.at[k, pl.ds(pl.multiple_of(low * half_cols + at * rows_x, SLOT), rows_x)]

    def first_gather(k, moves):
        wait(moves)
        total = rz[0, k].astype(F32)
        for o in range(1, nz // 2):
            total = total + rz[o, k].astype(F32)
        mine = piece(k, zlow, x)
        mine[...] = total.astype(BF)
        to_x = [send(mine, mine, (fi, z * nx + t)) for t in xpeers]
        return to_x, send(mine, mine, pair)

    def last_gather(k, moves):
        to_x, to_pair = moves
        rest = []
        if k % 2:
            to_pair.wait_recv()
            got = piece(k, 1 - zlow, x)
            rest = [send(got, got, (fi, z * nx + t)) for t in xpeers]
            return to_x + rest
        for o in range(1, nx):
            to_x[o - 1].wait_recv()
            got = piece(k, zlow, lax.rem(x - o + nx, nx))
            rest.append(send(got, got, pair))
        return [to_pair] + rest

    span = two.shape[0] // feat
    lanes_x = w // nx
    span_z = span // nz
    allz = [lax.rem(z + o, nz) for o in range(1, nz)]
    my_lanes = pl.ds(pl.multiple_of(x * lanes_x, 128), lanes_x)

    def layer_two():
        wait(rows_hidden)
        agg = table_mean(joined[:, :w], t2)
        joined[:, w:] = agg.astype(BF)
        both = joined[...]
        out[0] = dot(both, w_two[...]).astype(BF)
        two_part = dot(both.T, grads[...]).astype(BF)
        for f in range(feat):
            ts[f % 2, (f // 2) * span : (f // 2 + 1) * span] = two_part[f * span : (f + 1) * span]
        return send(ts.at[1 - c], u1, mate)

    def two_y(two_core):
        two_core.wait_recv()
        ub[...] = (ts[c].astype(F32) + u1[...].astype(F32)).astype(BF)
        return [
            send(ub.at[pl.ds(pl.multiple_of(lax.rem(y + o, ny) * span, SLOT), span)],
                 u2.at[o - 1], ypeers[o - 1])
            for o in range(1, ny)
        ]

    def two_x(moves):
        wait(moves)
        total = ub[pl.ds(pl.multiple_of(y * span, SLOT), span)].astype(F32)
        for o in range(ny - 1):
            total = total + u2[o].astype(F32)
        for t in range(nx):
            v[t] = total[:, t * lanes_x : (t + 1) * lanes_x].astype(BF)
        return [send(v.at[t], vx.at[o], (fi, z * nx + t)) for o, t in enumerate(xpeers)]

    def two_z(moves):
        wait(moves)
        total = v[x].astype(F32)
        for o in range(nx - 1):
            total = total + vx[o].astype(F32)
        vs[...] = total.astype(BF)
        return [
            send(vs.at[pl.ds(pl.multiple_of(t * span_z, SLOT), span_z)], vz.at[o], (fi, t * nx + x))
            for o, t in enumerate(allz)
        ]

    def two_zg(moves):
        wait(moves)
        total = vs[pl.ds(pl.multiple_of(z * span_z, SLOT), span_z)].astype(F32)
        for o in range(nz - 1):
            total = total + vz[o].astype(F32)
        mine = pl.ds(pl.multiple_of(fi * span + z * span_z, SLOT), span_z)
        two[mine, my_lanes] = total.astype(BF)
        piece = two.at[mine, my_lanes]
        return [send(piece, piece, (fi, t * nx + x)) for t in allz]

    def two_xg(moves):
        wait(moves)
        piece = two.at[pl.ds(pl.multiple_of(fi * span, SLOT), span), my_lanes]
        return [send(piece, piece, (fi, z * nx + t)) for t in xpeers]

    def two_yg(moves):
        wait(moves)
        piece = two.at[pl.ds(pl.multiple_of(fi * span, SLOT), span)]
        return [send(piece, piece, device) for device in ypeers], send(piece, piece, mate)

    def two_across(moves):
        across = []
        for o in range(1, ny):
            moves[o - 1].wait_recv()
            source = lax.rem(y - o + ny, ny) * 2 + c
            piece = two.at[pl.ds(pl.multiple_of(source * span, SLOT), span)]
            across.append(send(piece, piece, mate))
        return across

    moves = {}
    marks = [len(copies)]
    drained = 0
    for k in range(half):
        wait(gathers[k])
        moves[k] = chunk(k)
    two_core = layer_two()
    for k in range(half, chunks):
        gathers[k] = gather_end(k, *gathers[k])
    for k in range(half, chunks):
        wait(gathers[k])
        moves[k] = chunk(k)
        moves[k - half] = z_exchange(k - half, moves[k - half])
    two_moves = two_y(two_core)
    two_stages = [two_x, two_z, two_zg, two_xg]
    for step in range(1, chunks + 3):
        marks.append(len(copies))
        if half <= step < chunks:
            moves[step] = z_exchange(step, moves[step])
        if step >= 3:
            moves[step - 3] = last_gather(step - 3, moves[step - 3])
        if step <= chunks:
            moves[step - 1] = first_gather(step - 1, moves[step - 1])
        if step <= len(two_stages):
            two_moves = two_stages[step - 1](two_moves)
        elif step == len(two_stages) + 1:
            two_moves, two_mate = two_yg(two_moves)
        elif step == len(two_stages) + 2:
            two_moves = two_across(two_moves)
        settled = marks[max(step - 2, 0)]
        for copy in copies[drained:settled]:
            copy.wait_send()
        drained = settled
    for k in range(chunks):
        wait(moves[k])
    wait(two_moves)
    two_mate.wait_recv()
    for copy in copies[drained:]:
        copy.wait_send()


def finish(scale, out, one, two, out_hbm, one_hbm, two_hbm, one_wide, two_wide, sem):
    copies = [pltpu.make_async_copy(out, out_hbm, sem.at[0])]
    copies[0].start()
    for wide, target in ((one_wide, one_hbm), (two_wide, two_hbm)):
        rows = wide.shape[0] // 4
        for k in range(4):
            part = slice(k * rows, (k + 1) * rows)
            if wide is one_wide:
                for lane in range(one.shape[0]):
                    lanes = slice(lane * TILE, (lane + 1) * TILE)
                    wide[part, lanes] = one[lane, part].astype(F32) * scale
            else:
                wide[part] = two[part].astype(F32) * scale
            copy = pltpu.make_async_copy(wide.at[part], target.at[part], sem.at[len(copies)])
            copy.start()
            copies.append(copy)
    for copy in copies:
        copy.wait()


def on_device(nx, nz, features, w_one, w_two, neighbor, degree, send_rows, grad_out):
    feat, n, cols = features.shape
    w = w_two.shape[1]
    ny = feat // 2
    parts, kmax = send_rows.shape[1:]
    edge = parts * SLOT
    half_cols = cols // 2
    rows_x = half_cols // nx
    span = 2 * w // feat
    lanes_x = w // nx
    chunks = 2 * w // TILE
    n_copies = (
        2 + feat + 2 * (ny - 1) + 4 * (parts - 1)
        + chunks * (4 * ny + 2 + 4 * nx + nz)
        + 2 + 4 * ny + 2 * (nx + nz)
    )
    vm = pltpu.VMEM
    scratch = [
        vm(features.shape, BF), vm(w_one.shape, BF), vm(w_two.shape, BF),
        vm((neighbor.shape[2], 1, n), jnp.int32), vm((1, n), jnp.int32),
        vm((parts, kmax), jnp.int32), vm((n, w), BF),
        vm((2, 2, ny * n, w), F32), vm((2, 2, ny * n, w), BF), vm((2, ny * n, w), BF),
        vm((2, n, w), F32), vm((2, ny, n, w), BF), vm((2, ny - 1, n, w), BF),
        vm((n, n), BF), vm((n, n), BF), vm((2, n, edge), BF), vm((2, edge, n), BF),
        vm((2, edge, n), BF), vm((2, n, edge), BF),
        vm((edge, w // 2), BF), vm((edge, w // 2), BF), vm((edge, w // 2), BF),
        vm((edge, w // 2), BF), vm((edge, w // 2), BF), vm((edge, w // 2), BF),
        vm((edge, w // 2), BF), vm((edge, w // 2), BF),
        vm((n, 1), F32), vm((n, w), F32), vm((n, w), F32), vm((n, w), F32), vm((n, w), F32),
        vm((n, 2 * w), BF), vm((feat, n, half_cols), BF), vm((2, half_cols, feat * n), BF),
        vm((2, feat, chunks, n, TILE), BF),
        vm((chunks, half_cols, TILE), BF), vm((nx - 1, chunks, rows_x, TILE), BF),
        vm((nz // 2, chunks, rows_x, TILE), BF),
        vm((2, ny * span, w), BF), vm((ny * span, w), BF), vm((ny * span, w), BF),
        vm((ny - 1, span, w), BF), vm((nx, span, lanes_x), BF), vm((nx - 1, span, lanes_x), BF),
        vm((span, lanes_x), BF), vm((nz - 1, span // nz, lanes_x), BF),
        pltpu.SemaphoreType.DMA((n_copies,)), pltpu.SemaphoreType.DMA((n_copies,)),
        pltpu.SemaphoreType.DMA((8,)),
    ]
    spec = pl.BlockSpec(memory_space=pltpu.VMEM)
    hbm = pl.BlockSpec(memory_space=pltpu.HBM)
    out, one_sum, two_sum = pl.pallas_call(
        functools.partial(kernel, feat, nx, nz, kmax),
        out_shape=(
            jax.ShapeDtypeStruct((1, n, w), BF),
            jax.ShapeDtypeStruct((chunks, cols, TILE), BF),
            jax.ShapeDtypeStruct((2 * w, w), BF),
        ),
        in_specs=[hbm] * 7,
        out_specs=(spec, spec, spec),
        scratch_shapes=scratch,
        compiler_params=pltpu.CompilerParams(
            collective_id=0, has_side_effects=True, vmem_limit_bytes=40 * 1024 * 1024
        ),
    )(*(
        pltpu.with_memory_space_constraint(operand, pltpu.HBM)
        for operand in (
            features, w_one, w_two, jnp.transpose(neighbor, (2, 0, 1)), degree, send_rows[0],
            grad_out[0],
        )
    ))
    scale = 1.0 / math.sqrt(feat * n * parts)
    wide = (
        jax.ShapeDtypeStruct(out.shape, BF),
        jax.ShapeDtypeStruct((cols, 2 * w), F32),
        jax.ShapeDtypeStruct(two_sum.shape, F32),
    )
    return pl.pallas_call(
        functools.partial(finish, scale),
        out_shape=wide,
        in_specs=[spec] * 3,
        out_specs=(hbm, hbm, hbm),
        scratch_shapes=[
            vm((cols, 2 * w), F32), vm(two_sum.shape, F32), pltpu.SemaphoreType.DMA((9,)),
        ],
        compiler_params=pltpu.CompilerParams(vmem_limit_bytes=16 * 1024 * 1024),
    )(out, one_sum, two_sum)


def solution(mesh):
    parts = mesh.shape["dom"]
    nx = 1 << ((parts.bit_length() - 2) // 2)
    in_specs = (
        P(None, "dom", "feat"),
        P("feat", None),
        P(),
        P("feat", "dom", None),
        P("feat", "dom"),
        P("feat", "dom", None),
        P("feat", "dom", None),
    )
    out_specs = (P("feat", "dom", None), P("feat", None), P())
    return jax.shard_map(
        functools.partial(on_device, nx, parts // nx),
        mesh=mesh, in_specs=in_specs, out_specs=out_specs, check_vma=False,
    )
```

```python
import functools
import math

import jax
import jax.numpy as jnp
from jax import lax
from jax.experimental import pallas as pl
from jax.experimental.pallas import tpu as pltpu
from jax.sharding import PartitionSpec as P

BF = jnp.bfloat16
F32 = jnp.float32
SLOT = 16
TILE = 128
BROAD = 256


def dot(a, b):
    return jnp.dot(a, b, preferred_element_type=F32)


def dot_nt(a, b):
    return lax.dot_general(a, b, (((1,), (1,)), ((), ())), preferred_element_type=F32)


def kernel(
    feat, nx, nz, kmax,
    feats_hbm, w_one_hbm, w_two_hbm, nbr_hbm, deg_hbm, sends_hbm, grads_hbm,
    out, one, two,
    feats, w_one, w_two, nbr, deg, sends, grads,
    proj, projb, r1, q, qb, r2, cm, ct, cf, cft, sm, st, t1, t2, b1, b2, k0, k1, h0, h1,
    inv, dcs, dh, pself, dnl, joined, fx, ft, dp, g, rx, rz, ts, u1, ub, u2, v, vx, vs, vz,
    ssem, rsem, lsem,
):
    ny = feat // 2
    parts = nx * nz
    n = nbr.shape[2]
    w = grads.shape[1]
    cols = w_one.shape[0]
    fan = nbr.shape[0]
    half_cols = cols // 2
    fi = lax.axis_index("feat")
    di = lax.axis_index("dom")
    y, c = fi // 2, fi % 2
    z, x = di // nx, di % nx
    mate = (y * 2 + 1 - c, di)
    zlow, zhigh = z % 2, z // 2
    pair = (fi, (z + 1 - 2 * zlow) * nx + x)
    count = [0]

    def send(src, dst, device):
        k = count[0]
        count[0] += 1
        copy = pltpu.make_async_remote_copy(
            src_ref=src, dst_ref=dst, send_sem=ssem.at[k], recv_sem=rsem.at[k],
            device_id=device, device_id_type=pl.DeviceIdType.MESH,
        )
        copy.start()
        copies.append(copy)
        return copy

    copies = []
    ypeers = [(lax.rem(y + o, ny) * 2 + c, di) for o in range(1, ny)]
    dpeers = [lax.rem(di + o, parts) for o in range(1, parts)]
    xpeers = [lax.rem(x + o, nx) for o in range(1, nx)]
    zpeers = [lax.rem(zhigh + o, nz // 2) * 2 + zlow for o in range(1, nz // 2)]

    barrier = pltpu.get_barrier_semaphore()
    everyone = [mate] + ypeers + [(fi, p) for p in dpeers]
    for device in everyone:
        pl.semaphore_signal(barrier, inc=1, device_id=device, device_id_type=pl.DeviceIdType.MESH)

    def load(k, src, dst):
        copy = pltpu.make_async_copy(src, dst, lsem.at[k])
        copy.start()
        return copy

    first_loads = [load(0, w_one_hbm.at[:, w:], w_one.at[:, w:]), load(1, feats_hbm, feats)]
    self_load = load(2, w_one_hbm.at[:, :w], w_one.at[:, :w])
    later_loads = [
        load(3, nbr_hbm, nbr), load(4, deg_hbm, deg), load(5, sends_hbm, sends),
        load(6, grads_hbm, grads), load(7, w_two_hbm, w_two),
    ]

    def project(h):
        flat = feats[...].reshape(feat * n, cols)
        for t in range(w // BROAD):
            acc = dot(flat, w_one[:, h * w + t * BROAD : h * w + (t + 1) * BROAD])
            for f in range(feat):
                part = acc[f * n : (f + 1) * n]
                rows = slice((f // 2) * n, (f // 2 + 1) * n)
                lanes = slice(t * BROAD, (t + 1) * BROAD)
                proj[h, f % 2, rows, lanes] = part
                projb[h, f % 2, rows, lanes] = part.astype(BF)

    def core_send(h):
        return send(projb.at[h, 1 - c], r1.at[h], mate)

    def y_send(h):
        for j in range(ny):
            rows = slice(j * n, (j + 1) * n)
            qb[h, j] = (proj[h, c, rows] + r1[h, rows].astype(F32)).astype(BF)
        mine = pl.ds(pl.multiple_of(y * n, n), n)
        q[h] = proj[h, c, mine] + r1[h, mine].astype(F32)
        return [
            send(qb.at[h, lax.rem(y + o, ny)], r2.at[h, o - 1], ypeers[o - 1])
            for o in range(1, ny)
        ]

    def owned(h):
        total = q[h]
        for o in range(ny - 1):
            total = total + r2[h, o].astype(F32)
        return total

    def wait(items):
        for item in items:
            item.wait_recv()

    def slot(p):
        return pl.ds(pl.multiple_of(p * SLOT, SLOT), SLOT)

    wide = w // 2

    def trade_rows(values, boxes, table):
        boxes[...] = (dot(sm[0], values[:, :wide]) + dot(sm[1], values[:, wide:])).astype(BF)
        table[slot(di)] = boxes[slot(di)]
        return [send(boxes.at[slot(p)], table.at[slot(di)], (fi, p)) for p in dpeers]

    def table_mean(values, table):
        rows = table[...]
        far = jnp.concatenate([dot(cf[0], rows), dot(cf[1], rows)], axis=1)
        return (dot(cm[...], values) + far) * inv[...]

    def trade_back(values, outgoing, returned):
        scaled = (values * inv[...]).astype(BF)
        outgoing[...] = (
            dot(cft[0], scaled[:, :wide]) + dot(cft[1], scaled[:, wide:])
        ).astype(BF)
        returned[slot(di)] = outgoing[slot(di)]
        moves = [send(outgoing.at[slot(p)], returned.at[slot(di)], (fi, p)) for p in dpeers]
        return dot(ct[...], scaled), moves

    def come_home(returned):
        rows = returned[...]
        return jnp.concatenate([dot(st[0], rows), dot(st[1], rows)], axis=1)

    def pass_on(low, f, k, device):
        block = dp.at[low, f, k]
        return send(block, block, device)

    def y_source(o):
        return lax.rem(y - o + ny, ny) * 2 + c

    def gather_start(k):
        to_pair = pass_on(zlow, fi, k, pair)
        to_y = [pass_on(zlow, fi, k, device) for device in ypeers]
        return [to_pair], to_y, [pass_on(zlow, fi, k, mate)]

    def gather_forward(k, to_pair, to_y, to_mate):
        if k % 2:
            to_pair[0].wait_recv()
            far = [pass_on(1 - zlow, fi, k, device) for device in ypeers]
            to_mate.append(pass_on(1 - zlow, fi, k, mate))
            return far, to_y, to_mate
        for o in range(1, ny):
            to_y[o - 1].wait_recv()
            to_pair.append(pass_on(zlow, y_source(o), k, pair))
            to_mate.append(pass_on(zlow, y_source(o), k, mate))
        return to_pair, to_y, to_mate

    def gather_end(k, later, to_y, to_mate):
        if k % 2:
            for low, moves in ((zlow, to_y), (1 - zlow, later)):
                for o in range(1, ny):
                    moves[o - 1].wait_recv()
                    to_mate.append(pass_on(low, y_source(o), k, mate))
            return to_mate
        for o in range(ny):
            later[o].wait_recv()
            to_mate.append(pass_on(1 - zlow, y_source(o), k, mate))
        return to_mate

    first_loads[1].wait()
    pl.semaphore_wait(barrier, len(everyone))
    far_cols = pl.ds(pl.multiple_of((1 - zlow) * half_cols, 128), half_cols)
    near_cols = pl.ds(pl.multiple_of(zlow * half_cols, 128), half_cols)
    def send_features(f):
        return send(feats.at[f, :, far_cols], fx.at[f], pair)

    features_moves = [send_features(f) for f in range(feat // 2)]
    first_loads[0].wait()
    project(1)
    near_core = core_send(1)
    self_load.wait()
    project(0)
    self_core = core_send(0)
    near_core.wait_recv()
    near_y = y_send(1)
    self_core.wait_recv()
    self_y = y_send(0)

    for item in later_loads:
        item.wait()
    eye = lax.broadcasted_iota(jnp.int32, (n, n), 0) == lax.broadcasted_iota(jnp.int32, (n, n), 1)
    inv[...] = 1.0 / jnp.sum(jnp.where(eye, deg[...].astype(F32), 0.0), axis=1, keepdims=True)
    def tally(code):
        total = jnp.zeros(code.shape, F32)
        for s in range(fan):
            used = jnp.where(s < deg[...], nbr[s], -1)
            total = total + jnp.where(used == code, 1.0, 0.0)
        return total

    own = tally(lax.broadcasted_iota(jnp.int32, (n, n), 0))
    ct[...] = own.astype(BF)
    cm[...] = own.T.astype(BF)
    entry = lax.broadcasted_iota(jnp.int32, (parts * SLOT, n), 0)
    for h in range(2):
        k = (entry & 15) - h * kmax
        far = tally(jnp.where((k >= 0) & (k < kmax), n + (entry >> 4) * kmax + k, -2))
        cft[h] = far.astype(BF)
        cf[h] = far.T.astype(BF)
    edge = (parts * SLOT, parts)
    owner = lax.broadcasted_iota(jnp.int32, edge, 0) >> 4 == lax.broadcasted_iota(jnp.int32, edge, 1)
    spread_rows = dot(jnp.where(owner, 1.0, 0.0).astype(BF), sends[...].astype(F32).astype(BF))
    place = (parts * SLOT, kmax)
    spot = lax.broadcasted_iota(jnp.int32, place, 0) & 15
    lane = lax.broadcasted_iota(jnp.int32, (parts * SLOT, n), 1).astype(F32)
    for h in range(2):
        here = spot == lax.broadcasted_iota(jnp.int32, place, 1) + h * kmax
        chosen = jnp.sum(jnp.where(here, spread_rows + 1.0, 0.0), axis=1, keepdims=True) - 1.0
        picks = jnp.where(chosen == lane, 1.0, 0.0)
        sm[h] = picks.astype(BF)
        st[h] = picks.T.astype(BF)
    dcat = dot_nt(grads[...], w_two[...])
    dcs[...] = dcat[:, :w]
    local, back_agg = trade_back(dcat[:, w:], k0, h0)
    dcs[...] += local

    wait(near_y)
    p_near = owned(1).astype(BF)
    rows_near = trade_rows(p_near, b1, t1)
    features_moves += [send_features(f) for f in range(feat // 2, feat)]
    ft[zlow] = feats[:, :, near_cols].reshape(feat * n, half_cols).T
    wait(self_y)
    pself[...] = owned(0)
    wait(back_agg)
    dh[...] = dcs[...] + come_home(h0)
    wait(rows_near)
    pre = pself[...] + table_mean(p_near, t1)
    sig = 1.0 / (1.0 + jnp.exp(-pre))
    d_pre = dh[...] * sig * (1.0 + pre * (1.0 - sig))
    chunks = 2 * w // TILE
    half = chunks // 2
    for k in range(half):
        dp[zlow, fi, k] = d_pre[:, k * TILE : (k + 1) * TILE].astype(BF)
    gathers = {}
    near_local, back_pre = trade_back(d_pre, k1, h1)
    dnl[...] = near_local
    for k in range(half):
        gathers[k] = gather_start(k)
    hidden = (pre * sig).astype(BF)
    joined[:, :w] = hidden
    rows_hidden = trade_rows(hidden, b2, t2)

    wait(features_moves)
    ft[1 - zlow] = fx[...].reshape(feat * n, half_cols).T
    wait(back_pre)
    d_near = (dnl[...] + come_home(h1)).astype(BF)
    for k in range(half):
        dp[zlow, fi, half + k] = d_near[:, k * TILE : (k + 1) * TILE]
    for k in range(half, chunks):
        gathers[k] = gather_start(k)
    for k in range(half):
        gathers[k] = gather_forward(k, *gathers[k])

    for k in range(half, chunks):
        gathers[k] = gather_forward(k, *gathers[k])
    for k in range(half):
        gathers[k] = gather_end(k, *gathers[k])

    rows_x = half_cols // nx

    def chunk(k):
        g[k] = (
            dot(ft[0], dp[0, :, k].reshape(feat * n, TILE))
            + dot(ft[1], dp[1, :, k].reshape(feat * n, TILE))
        ).astype(BF)
        return [
            send(g.at[k, pl.ds(pl.multiple_of(t * rows_x, SLOT), rows_x)], rx.at[o, k],
                 (fi, z * nx + t))
            for o, t in enumerate(xpeers)
        ]

    def z_exchange(k, moves):
        wait(moves)
        total = g[k, pl.ds(pl.multiple_of(x * rows_x, SLOT), rows_x)].astype(F32)
        for o in range(nx - 1):
            total = total + rx[o, k].astype(F32)
        rz[zhigh, k] = total.astype(BF)
        part = rz.at[zhigh, k]
        return [send(part, part, (fi, t * nx + x)) for t in zpeers]

    def piece(k, low, at):
        return one.at[k, pl.ds(pl.multiple_of(low * half_cols + at * rows_x, SLOT), rows_x)]

    def first_gather(k, moves):
        wait(moves)
        total = rz[0, k].astype(F32)
        for o in range(1, nz // 2):
            total = total + rz[o, k].astype(F32)
        mine = piece(k, zlow, x)
        mine[...] = total.astype(BF)
        to_x = [send(mine, mine, (fi, z * nx + t)) for t in xpeers]
        return to_x, send(mine, mine, pair)

    def last_gather(k, moves):
        to_x, to_pair = moves
        rest = []
        if k % 2:
            to_pair.wait_recv()
            got = piece(k, 1 - zlow, x)
            rest = [send(got, got, (fi, z * nx + t)) for t in xpeers]
            return to_x + rest
        for o in range(1, nx):
            to_x[o - 1].wait_recv()
            got = piece(k, zlow, lax.rem(x - o + nx, nx))
            rest.append(send(got, got, pair))
        return [to_pair] + rest

    span = two.shape[0] // feat
    lanes_x = w // nx
    span_z = span // nz
    allz = [lax.rem(z + o, nz) for o in range(1, nz)]
    my_lanes = pl.ds(pl.multiple_of(x * lanes_x, 128), lanes_x)

    def layer_two():
        wait(rows_hidden)
        agg = table_mean(joined[:, :w], t2)
        joined[:, w:] = agg.astype(BF)
        both = joined[...]
        out[0] = dot(both, w_two[...]).astype(BF)
        two_part = dot(both.T, grads[...]).astype(BF)
        for f in range(feat):
            ts[f % 2, (f // 2) * span : (f // 2 + 1) * span] = two_part[f * span : (f + 1) * span]
        return send(ts.at[1 - c], u1, mate)

    def two_y(two_core):
        two_core.wait_recv()
        ub[...] = (ts[c].astype(F32) + u1[...].astype(F32)).astype(BF)
        return [
            send(ub.at[pl.ds(pl.multiple_of(lax.rem(y + o, ny) * span, SLOT), span)],
                 u2.at[o - 1], ypeers[o - 1])
            for o in range(1, ny)
        ]

    def two_x(moves):
        wait(moves)
        total = ub[pl.ds(pl.multiple_of(y * span, SLOT), span)].astype(F32)
        for o in range(ny - 1):
            total = total + u2[o].astype(F32)
        for t in range(nx):
            v[t] = total[:, t * lanes_x : (t + 1) * lanes_x].astype(BF)
        return [send(v.at[t], vx.at[o], (fi, z * nx + t)) for o, t in enumerate(xpeers)]

    def two_z(moves):
        wait(moves)
        total = v[x].astype(F32)
        for o in range(nx - 1):
            total = total + vx[o].astype(F32)
        vs[...] = total.astype(BF)
        return [
            send(vs.at[pl.ds(pl.multiple_of(t * span_z, SLOT), span_z)], vz.at[o], (fi, t * nx + x))
            for o, t in enumerate(allz)
        ]

    def two_zg(moves):
        wait(moves)
        total = vs[pl.ds(pl.multiple_of(z * span_z, SLOT), span_z)].astype(F32)
        for o in range(nz - 1):
            total = total + vz[o].astype(F32)
        mine = pl.ds(pl.multiple_of(fi * span + z * span_z, SLOT), span_z)
        two[mine, my_lanes] = total.astype(BF)
        piece = two.at[mine, my_lanes]
        return [send(piece, piece, (fi, t * nx + x)) for t in allz]

    def two_xg(moves):
        wait(moves)
        piece = two.at[pl.ds(pl.multiple_of(fi * span, SLOT), span), my_lanes]
        return [send(piece, piece, (fi, z * nx + t)) for t in xpeers]

    def two_yg(moves):
        wait(moves)
        piece = two.at[pl.ds(pl.multiple_of(fi * span, SLOT), span)]
        return [send(piece, piece, device) for device in ypeers], send(piece, piece, mate)

    def two_across(moves):
        across = []
        for o in range(1, ny):
            moves[o - 1].wait_recv()
            source = lax.rem(y - o + ny, ny) * 2 + c
            piece = two.at[pl.ds(pl.multiple_of(source * span, SLOT), span)]
            across.append(send(piece, piece, mate))
        return across

    moves = {}
    marks = [len(copies)]
    drained = 0
    for k in range(half):
        wait(gathers[k])
        moves[k] = chunk(k)
    two_core = layer_two()
    for k in range(half, chunks):
        gathers[k] = gather_end(k, *gathers[k])
    for k in range(half, chunks):
        wait(gathers[k])
        moves[k] = chunk(k)
        moves[k - half] = z_exchange(k - half, moves[k - half])
    two_moves = two_y(two_core)
    two_stages = [two_x, two_z, two_zg, two_xg]
    for step in range(1, chunks + 3):
        marks.append(len(copies))
        if half <= step < chunks:
            moves[step] = z_exchange(step, moves[step])
        if step >= 3:
            moves[step - 3] = last_gather(step - 3, moves[step - 3])
        if step <= chunks:
            moves[step - 1] = first_gather(step - 1, moves[step - 1])
        if step <= len(two_stages):
            two_moves = two_stages[step - 1](two_moves)
        elif step == len(two_stages) + 1:
            two_moves, two_mate = two_yg(two_moves)
        elif step == len(two_stages) + 2:
            two_moves = two_across(two_moves)
        settled = marks[max(step - 2, 0)]
        for copy in copies[drained:settled]:
            copy.wait_send()
        drained = settled
    for k in range(chunks):
        wait(moves[k])
    wait(two_moves)
    two_mate.wait_recv()
    for copy in copies[drained:]:
        copy.wait_send()


def finish(scale, out, one, two, out_hbm, one_hbm, two_hbm, one_wide, two_wide, sem):
    copies = [pltpu.make_async_copy(out, out_hbm, sem.at[0])]
    copies[0].start()
    for wide, target in ((one_wide, one_hbm), (two_wide, two_hbm)):
        rows = wide.shape[0] // 4
        for k in range(4):
            part = slice(k * rows, (k + 1) * rows)
            if wide is one_wide:
                for lane in range(one.shape[0]):
                    lanes = slice(lane * TILE, (lane + 1) * TILE)
                    wide[part, lanes] = one[lane, part].astype(F32) * scale
            else:
                wide[part] = two[part].astype(F32) * scale
            copy = pltpu.make_async_copy(wide.at[part], target.at[part], sem.at[len(copies)])
            copy.start()
            copies.append(copy)
    for copy in copies:
        copy.wait()


def on_device(nx, nz, features, w_one, w_two, neighbor, degree, send_rows, grad_out):
    feat, n, cols = features.shape
    w = w_two.shape[1]
    ny = feat // 2
    parts, kmax = send_rows.shape[1:]
    edge = parts * SLOT
    half_cols = cols // 2
    rows_x = half_cols // nx
    span = 2 * w // feat
    lanes_x = w // nx
    chunks = 2 * w // TILE
    n_copies = (
        2 + feat + 2 * (ny - 1) + 4 * (parts - 1)
        + chunks * (4 * ny + 2 + 4 * nx + nz)
        + 2 + 4 * ny + 2 * (nx + nz)
    )
    vm = pltpu.VMEM
    scratch = [
        vm(features.shape, BF), vm(w_one.shape, BF), vm(w_two.shape, BF),
        vm((neighbor.shape[2], 1, n), jnp.int32), vm((1, n), jnp.int32),
        vm((parts, kmax), jnp.int32), vm((n, w), BF),
        vm((2, 2, ny * n, w), F32), vm((2, 2, ny * n, w), BF), vm((2, ny * n, w), BF),
        vm((2, n, w), F32), vm((2, ny, n, w), BF), vm((2, ny - 1, n, w), BF),
        vm((n, n), BF), vm((n, n), BF), vm((2, n, edge), BF), vm((2, edge, n), BF),
        vm((2, edge, n), BF), vm((2, n, edge), BF),
        vm((edge, w // 2), BF), vm((edge, w // 2), BF), vm((edge, w // 2), BF),
        vm((edge, w // 2), BF), vm((edge, w // 2), BF), vm((edge, w // 2), BF),
        vm((edge, w // 2), BF), vm((edge, w // 2), BF),
        vm((n, 1), F32), vm((n, w), F32), vm((n, w), F32), vm((n, w), F32), vm((n, w), F32),
        vm((n, 2 * w), BF), vm((feat, n, half_cols), BF), vm((2, half_cols, feat * n), BF),
        vm((2, feat, chunks, n, TILE), BF),
        vm((chunks, half_cols, TILE), BF), vm((nx - 1, chunks, rows_x, TILE), BF),
        vm((nz // 2, chunks, rows_x, TILE), BF),
        vm((2, ny * span, w), BF), vm((ny * span, w), BF), vm((ny * span, w), BF),
        vm((ny - 1, span, w), BF), vm((nx, span, lanes_x), BF), vm((nx - 1, span, lanes_x), BF),
        vm((span, lanes_x), BF), vm((nz - 1, span // nz, lanes_x), BF),
        pltpu.SemaphoreType.DMA((n_copies,)), pltpu.SemaphoreType.DMA((n_copies,)),
        pltpu.SemaphoreType.DMA((8,)),
    ]
    spec = pl.BlockSpec(memory_space=pltpu.VMEM)
    hbm = pl.BlockSpec(memory_space=pltpu.HBM)
    out, one_sum, two_sum = pl.pallas_call(
        functools.partial(kernel, feat, nx, nz, kmax),
        out_shape=(
            jax.ShapeDtypeStruct((1, n, w), BF),
            jax.ShapeDtypeStruct((chunks, cols, TILE), BF),
            jax.ShapeDtypeStruct((2 * w, w), BF),
        ),
        in_specs=[hbm] * 7,
        out_specs=(spec, spec, spec),
        scratch_shapes=scratch,
        compiler_params=pltpu.CompilerParams(
            collective_id=0, has_side_effects=True, vmem_limit_bytes=40 * 1024 * 1024
        ),
    )(*(
        pltpu.with_memory_space_constraint(operand, pltpu.HBM)
        for operand in (
            features, w_one, w_two, jnp.transpose(neighbor, (2, 0, 1)), degree, send_rows[0],
            grad_out[0],
        )
    ))
    scale = 1.0 / math.sqrt(feat * n * parts)
    wide = (
        jax.ShapeDtypeStruct(out.shape, BF),
        jax.ShapeDtypeStruct((cols, 2 * w), F32),
        jax.ShapeDtypeStruct(two_sum.shape, F32),
    )
    return pl.pallas_call(
        functools.partial(finish, scale),
        out_shape=wide,
        in_specs=[spec] * 3,
        out_specs=(hbm, hbm, hbm),
        scratch_shapes=[
            vm((cols, 2 * w), F32), vm(two_sum.shape, F32), pltpu.SemaphoreType.DMA((9,)),
        ],
        compiler_params=pltpu.CompilerParams(vmem_limit_bytes=16 * 1024 * 1024),
    )(out, one_sum, two_sum)


def solution(mesh):
    parts = mesh.shape["dom"]
    nx = 1 << ((parts.bit_length() - 2) // 2)
    in_specs = (
        P(None, "dom", "feat"),
        P("feat", None),
        P(),
        P("feat", "dom", None),
        P("feat", "dom"),
        P("feat", "dom", None),
        P("feat", "dom", None),
    )
    out_specs = (P("feat", "dom", None), P("feat", None), P())
    return jax.shard_map(
        functools.partial(on_device, nx, parts // nx),
        mesh=mesh, in_specs=in_specs, out_specs=out_specs, check_vma=False,
    )
```
